32 devices in a mesh: band: 2 (over x), ens: 16 (over z, y, core).
Axes of the slice: x: 2, y: 2, z: 4, core: 2. Of those that a mesh axis runs over, the one named last changes fastest.
Arguments:
- fine_state: bfloat16 [64, 8, 16, 512], P('ens', None, 'band'), may hold values from -5 to 5
- coarse_state: bfloat16 [64, 8, 4, 128], P('ens', None, 'band'), may hold values from -5 to 5
- noise: bfloat16 [2, 64, 8, 16, 512], P(None, 'ens', None, 'band'), may hold values from -5 to 5
- kernel_fine: bfloat16 [8, 72], replicated, may hold values from -0.75 to 0.75
- kernel_coarse: bfloat16 [8, 72], replicated, may hold values from -0.75 to 0.75
- obs_fine: bfloat16 [8, 16, 512], P(None, 'band'), may hold values from -5 to 6
- obs_coarse: bfloat16 [8, 4, 128], P(None, 'band'), may hold values from -5 to 6
- precision_fine: float32 [16], P('band'), may hold values from 0.3 to 14, as said below
- precision_coarse: float32 [4], P('band'), may hold values from 0.3 to 14, as said below
- offspring: int32 [64], replicated, may hold values from 0 to 8, as said below
- dest_slot: int32 [64], replicated, may hold values from 0 to 63, each once
Outputs:
- fine_next: bfloat16 [64, 8, 16, 512], P('ens', None, 'band')
- coarse_next: bfloat16 [64, 8, 4, 128], P('ens', None, 'band')
- logw_fine: float32 [64], P('ens')
- logw_coarse: float32 [64], P('ens')
The draws below stay inside these ranges and needn't reach their ends.
Inputs may be any that keep to these rules, and one draw needn't show every extreme that they name: non-negative offspring counts that sum to 64; the counts of each aligned block of 8 pairs sum to 8. `dest_slot`: each slot appears once. `precision_fine`: positive. `precision_coarse`: positive.
All inputs are finite; a program needn't handle non-finite values.
Results may differ from the reference program's by a relative error of at most 0.0049.
Values may be sent and summed in bfloat16 or wider, within the bound.
A program may use at most 64 MiB of HBM per device.

```python
import jax
import jax.numpy as jnp
from jax import lax

CH = 8
LON = 512
STEPS = 2
NLAT = 16
NLATC = 4
LONC = 128
PARTICLES = 64


def observed_field(key, shape):
    values = jnp.clip(jax.random.normal(key, shape, jnp.float32), -5.0, 5.0)
    return values.astype(jnp.bfloat16)


def draw_obs_fine(key, part):
    return observed_field(key, (CH, NLAT, LON))


def draw_obs_coarse(key, part):
    return observed_field(key, (CH, NLATC, LONC))


def rising_rows(key, count):
    rows = jnp.arange(count, dtype=jnp.float32) / jnp.float32(max(count - 1, 1))
    values = 3.0 ** rows * jax.random.uniform(key, (count,), jnp.float32, 0.7, 1.3)
    return values.astype(jnp.float32)


def draw_precision_fine(key, part):
    return rising_rows(key, NLAT)


def draw_precision_coarse(key, part):
    return rising_rows(key, NLATC)


def draw_offspring(key, part):
    groups = PARTICLES // 8
    picks = jax.random.randint(jax.random.fold_in(key, 11), (groups, 8), 0, 8)
    heavy = jax.random.randint(jax.random.fold_in(key, 12), (), 0, groups)
    target = jax.random.randint(jax.random.fold_in(key, 13), (), 0, 8)
    group_ids = jnp.arange(groups, dtype=jnp.int32)
    picks = jnp.where((group_ids == heavy)[:, None], target, picks).astype(jnp.int32)
    within = jnp.arange(8, dtype=jnp.int32)
    counts = jnp.sum((picks[:, :, None] == within[None, None, :]).astype(jnp.int32), axis=1)
    return counts.reshape(PARTICLES).astype(jnp.int32)


def block_levels(rng, extent, pieces, smallest, top_value):
    gain, own = 1.0, jax.random.fold_in(rng, 6)
    for axis_at, parts in pieces:
        steps = jnp.exp(jax.random.uniform(jax.random.fold_in(own, axis_at), (parts,), jnp.float32, smallest / len(pieces), top_value / len(pieces)))
        gain = gain * jnp.repeat(steps, extent[axis_at] // parts).reshape([-1 if axis == axis_at else 1 for axis in range(len(extent))])
    return gain


def normal_values(rng, shape, width, reach, cuts=(), kind=jnp.bfloat16):
    loudness = block_levels(rng, shape, cuts, -0.22, 0.18) if cuts else 1.0
    result = jax.random.normal(rng, shape, jnp.float32) * width * loudness
    return jnp.minimum(jnp.maximum(result, -reach), reach).astype(kind)


def setup_inputs(seed: int = 0) -> dict:
    keys = jax.random.split(jax.random.key(seed), 12)
    fine_state = normal_values(keys[0], (PARTICLES, CH, NLAT, LON), 1.0, 5.0, ((0, 16), (2, 2)))
    coarse_state = normal_values(keys[1], (PARTICLES, CH, NLATC, LONC), 1.0, 5.0, ((0, 16), (2, 2)))
    noise = normal_values(keys[2], (STEPS, PARTICLES, CH, NLAT, LON), 1.0, 5.0, ((1, 16), (3, 2)))
    kernel_fine = normal_values(keys[3], (CH, CH * 9), (CH * 9) ** -0.5, 0.75)
    kernel_coarse = normal_values(keys[4], (CH, CH * 9), (CH * 9) ** -0.5, 0.75)
    obs_fine = draw_obs_fine(jax.random.fold_in(keys[11], 71), 0)
    obs_coarse = draw_obs_coarse(jax.random.fold_in(keys[11], 71), 0)
    precision_fine = draw_precision_fine(jax.random.fold_in(keys[11], 71), 0)
    precision_coarse = draw_precision_coarse(jax.random.fold_in(keys[11], 71), 0)
    offspring = draw_offspring(jax.random.fold_in(keys[11], 71), 0)
    dest_slot = jax.random.permutation(keys[10], PARTICLES).astype(jnp.int32)
    return dict(fine_state=fine_state, coarse_state=coarse_state, noise=noise, kernel_fine=kernel_fine, kernel_coarse=kernel_coarse, obs_fine=obs_fine, obs_coarse=obs_coarse, precision_fine=precision_fine, precision_coarse=precision_coarse, offspring=offspring, dest_slot=dest_slot)


def conv_taps(state):
    rows = state.shape[1]
    padded = jnp.pad(state, ((0, 0), (1, 1), (0, 0)))
    stack = []
    for shift_row in range(3):
        band_rows = padded[:, shift_row:shift_row + rows, :]
        for shift_col in (-1, 0, 1):
            stack.append(jnp.roll(band_rows, -shift_col, axis=2))
    joined = jnp.stack(stack, axis=1)
    return joined.reshape(joined.shape[0] * 9, rows, joined.shape[3])

def advance(state, forcing, kernel):
    taps = conv_taps(state).astype(jnp.float32)
    mixed = jnp.einsum('ok,krl->orl', kernel.astype(jnp.float32), taps)
    return (state.astype(jnp.float32) + 0.5 * jnp.tanh(mixed + forcing)).astype(jnp.bfloat16)

def restrict(field):
    shape = field.shape
    blocks = field.reshape(shape[0], shape[1] // 4, 4, shape[2] // 4, 4)
    return 4.0 * lax.optimization_barrier(jnp.mean(blocks, axis=(2, 4)))

def misfit(state, observed, precision, scale):
    diff = state.astype(jnp.float32) - observed.astype(jnp.float32)
    return -0.5 * scale * jnp.sum(precision[None, :, None] * diff * diff)

def normalize(like):
    peak = jnp.max(like)
    return like - (peak + jnp.log(jnp.sum(jnp.exp(like - peak))))

def reference(fine_state, coarse_state, noise, kernel_fine, kernel_coarse, obs_fine, obs_coarse, precision_fine, precision_coarse, offspring, dest_slot):
    scale_fine = 1.0 / jnp.sqrt(jnp.float32(CH * NLAT * LON))
    scale_coarse = 1.0 / jnp.sqrt(jnp.float32(CH * NLATC * LONC))

    def one_pair(items):
        fine, coarse, forcing = items
        for step in range(STEPS):
            force = forcing[step].astype(jnp.float32)
            fine = advance(fine, force, kernel_fine)
            coarse = advance(coarse, restrict(force), kernel_coarse)
        like_f = misfit(fine, obs_fine, precision_fine, scale_fine)
        like_c = misfit(coarse, obs_coarse, precision_coarse, scale_coarse)
        return (fine, coarse, like_f, like_c)
    forcing_all = jnp.swapaxes(noise, 0, 1)
    fine_fc, coarse_fc, like_fine, like_coarse = lax.map(one_pair, (fine_state, coarse_state, forcing_all))
    logw_fine = normalize(like_fine)
    logw_coarse = normalize(like_coarse)
    order = jnp.arange(PARTICLES, dtype=jnp.int32)
    ends = jnp.cumsum(offspring).astype(jnp.int32)
    parent = lax.optimization_barrier(jnp.sum((ends[None, :] <= order[:, None]).astype(jnp.int32), axis=1)).astype(jnp.int32)
    slot_parent = lax.optimization_barrier(jnp.sum(jnp.where(dest_slot[None, :] == order[:, None], parent[None, :], 0), axis=1)).astype(jnp.int32)
    fine_next = fine_fc[slot_parent]
    coarse_next = coarse_fc[slot_parent]
    return (fine_next, coarse_next, logw_fine, logw_coarse)
```

```python
import functools
import math

import jax
import jax.numpy as jnp
from jax import lax
from jax.experimental import pallas as pl
from jax.experimental.pallas import tpu as pltpu
from jax.sharding import PartitionSpec as P

F32 = jnp.float32
BF16 = jnp.bfloat16
I32 = jnp.int32
TILE_R = 16
TILE_L = 128


def iota(shape, dim):
    return lax.broadcasted_iota(I32, shape, dim)


def onehot(cond):
    return jnp.where(cond, 1.0, 0.0).astype(BF16)


def mm(a, b):
    return jnp.dot(a, b, preferred_element_type=F32)


def layout(idx, ch, rows, halo):
    base = ch * rows
    own_c, own_r = idx >> int(math.log2(rows)), idx & (rows - 1)
    if halo == 0:
        return own_c, own_r
    up = idx - base
    down = up - halo * ch
    above = -1 - jnp.where(up >= ch, 1, 0)
    below = rows + jnp.where(down >= ch, 1, 0)
    side_c = up & (ch - 1)
    side_r = jnp.where(down < 0, above, below)
    return jnp.where(idx < base, own_c, side_c), jnp.where(idx < base, own_r, side_r)


def conv_matrix(kern, ch, rows, halo_out, halo_in):
    n_out = ch * (rows + 2 * halo_out)
    n_in = ch * (rows + 2 * halo_in)
    o, r_out = layout(iota((n_out, 1), 0), ch, rows, halo_out)
    col = iota((1, 3 * n_in), 1)
    shift = jnp.where(col >= n_in, 1, 0) + jnp.where(col >= 2 * n_in, 1, 0)
    i, r_in = layout(col - n_in * shift, ch, rows, halo_in)
    spread = mm(onehot(o == iota((n_out, ch), 1)), kern).astype(BF16)
    taps = iota((9 * ch, 3 * n_in), 0)
    total = None
    for a in range(3):
        pick = mm(spread, onehot(taps == 9 * i + 3 * a + shift))
        term = jnp.where(r_in - r_out + 1 == a, pick, 0.0)
        total = term if total is None else total + term
    return total.astype(BF16)


def shifted(x, width):
    parts = [x[:, j : j + width] for j in range(0, x.shape[1], width)]
    left = [pltpu.roll(v, 1, 1) for v in parts]
    right = [pltpu.roll(v, width - 1, 1) for v in parts]
    join = lambda vs: vs[0] if len(vs) == 1 else jnp.concatenate(vs, axis=1)
    return jnp.concatenate([join(left), x, join(right)], axis=0).astype(BF16)


def kernel(
    bands, members,
    fine, coarse, noise, kf, kc, obs_f, obs_c, prec_f, prec_c, offs, dest,
    out_f, out_c, out_lf, out_lc,
    halo_tx, halo_rx, edge_tx, edge_rx, fin, recv1, chosen, cstage, recvc, cchosen, recvc2,
    likeb, likee, par_v, par_s,
    h_send, h_recv, e_send, e_recv, s1, r1, s2, r2, cs1, cr1, cs2, cr2, bs, br, ls, lr, loc,
):
    band = lax.axis_index("band")
    me = lax.axis_index("ens")
    n_p, ch, hf, lon = fine.shape[0], kf.shape[0], prec_f.shape[1], fine.shape[2]
    hc, lonc = prec_c.shape[1], coarse.shape[1]
    rf, rc = ch * hf, ch * hc
    lane_blocks = lon // TILE_L
    shares = (rf // TILE_R) * lane_blocks
    holders = n_p * rc // TILE_R
    piece = rc // holders
    total = offs.shape[1]
    group = (me // shares) * shares
    rank = me - group

    def holder(c):
        return c * (shares // holders) + (c % 2) * (shares // holders // 2)

    def tile(ref, share):
        row = pl.multiple_of((share // lane_blocks) * TILE_R, TILE_R)
        lane = pl.multiple_of((share % lane_blocks) * TILE_L, TILE_L)
        return ref.at[:, pl.ds(row, TILE_R), pl.ds(lane, TILE_L)]

    def copy_to(src, dst, send, recv, device):
        return pltpu.make_async_remote_copy(
            src_ref=src, dst_ref=dst, send_sem=send, recv_sem=recv,
            device_id=device, device_id_type=pl.DeviceIdType.MESH,
        )

    barrier = pltpu.get_barrier_semaphore()
    for k in range(1, members):
        pl.semaphore_signal(barrier, inc=1, device_id={"ens": lax.rem(me + k, members)},
                            device_id_type=pl.DeviceIdType.MESH)
    for k in range(1, bands):
        pl.semaphore_signal(barrier, inc=1, device_id={"band": lax.rem(band + k, bands)},
                            device_id_type=pl.DeviceIdType.MESH)

    def edge_rows(n_side, rows):
        q = iota((2 * n_side, ch * rows), 0)
        lower = q >= n_side
        t = jnp.where(lower, q - n_side, q)
        depth = jnp.where(t >= ch, 1, 0)
        row = jnp.where(lower, rows - 1 - depth, depth)
        return onehot(iota((2 * n_side, ch * rows), 1) == (t & (ch - 1)) * rows + row)

    sel_state, sel_noise, sel_coarse = edge_rows(2 * ch, hf), edge_rows(ch, hf), edge_rows(2 * ch, hc)
    n_base = n_p * 2 * ch
    c_base = n_base + n_p * ch
    picked_noise = []
    for p in range(n_p):
        rows = mm(sel_state, fine[p]).astype(BF16)
        halo_tx[0, pl.ds(p * 2 * ch, 2 * ch), :] = rows[: 2 * ch]
        halo_tx[1, pl.ds(p * 2 * ch, 2 * ch), :] = rows[2 * ch :]
        picked_noise.append(mm(sel_noise, noise[0, p]))
    for side in range(2):
        halo_tx[side, pl.ds(n_base, n_p * ch), :] = jnp.concatenate(
            [v[side * ch : (side + 1) * ch] for v in picked_noise], axis=0
        ).astype(BF16)
    c0 = jnp.concatenate([coarse[pl.ds(p * rc, rc), :] for p in range(n_p)], axis=1)
    rows = mm(sel_coarse, c0).astype(BF16)
    halo_tx[0, pl.ds(c_base, 2 * ch), :] = rows[: 2 * ch]
    halo_tx[1, pl.ds(c_base, 2 * ch), :] = rows[2 * ch :]

    pl.semaphore_wait(barrier, members + bands - 2)

    up, down = lax.max(band - 1, 0), lax.min(band + 1, bands - 1)
    has_up, has_down = band > 0, band < bands - 1

    def pair(tx, rx, send, recv, side):
        return copy_to(tx.at[side], rx.at[1 - side], send.at[side], recv.at[1 - side],
                       {"band": up if side == 0 else down})

    halo = [pair(halo_tx, halo_rx, h_send, h_recv, side) for side in range(2)]
    edge = [pair(edge_tx, edge_rx, e_send, e_recv, side) for side in range(2)]

    @pl.when(has_up)
    def _():
        halo[0].start()

    @pl.when(has_down)
    def _():
        halo[1].start()

    r4 = hf // hc
    q = iota((rc + 2 * ch, rf), 0)
    cell_c = jnp.where(q < rc, q >> int(math.log2(hc)), (q - rc) & (ch - 1))
    cell_r = jnp.where(q < rc, q & (hc - 1), jnp.where(q < rc + ch, 0, hc - 1))
    src = iota((rc + 2 * ch, rf), 1)
    gather_rows = onehot((src >> int(math.log2(r4))) == cell_c * hc + cell_r)
    l4 = lon // lonc
    fold = onehot((iota((lon, lonc), 0) >> int(math.log2(l4))) == iota((lon, lonc), 1))
    sums = jnp.concatenate(
        [mm(gather_rows, noise[s, p]) for s in range(2) for p in range(n_p)], axis=0
    )
    hi = sums.astype(BF16)
    rest = sums - hi.astype(F32)
    mid = rest.astype(BF16)
    low = (rest - mid.astype(F32)).astype(BF16)
    scale_r = 4.0 / (r4 * l4)
    folded = (mm(hi, fold) + (mm(mid, fold) + mm(low, fold))) * scale_r
    block = rc + 2 * ch

    def forcing_rows(step, lo, n):
        return jnp.concatenate(
            [folded[(step * n_p + p) * block + lo : (step * n_p + p) * block + lo + n] for p in range(n_p)],
            axis=1,
        )

    edge_tx[0] = forcing_rows(0, rc, ch)
    edge_tx[1] = forcing_rows(0, rc + ch, ch)

    @pl.when(has_up)
    def _():
        edge[0].start()

    @pl.when(has_down)
    def _():
        edge[1].start()

    lane_w = par_v.shape[1]
    lanes = iota((total, total), 1)
    subs = iota((total, total), 0)
    ends = jnp.sum(jnp.where(lanes <= subs, offs[...], 0), axis=1, keepdims=True)
    parent = jnp.sum(jnp.where(ends <= lanes, 1, 0), axis=0, keepdims=True)
    slot_col = jnp.sum(jnp.where(dest[...] == subs, parent, 0), axis=1, keepdims=True)
    par_v[...] = jnp.sum(
        jnp.where(iota((total, lane_w), 0) == iota((total, lane_w), 1), jnp.minimum(slot_col, total - 1), 0),
        axis=0, keepdims=True,
    )
    to_smem = pltpu.make_async_copy(par_v, par_s, loc.at[0])
    to_smem.start()

    w1 = conv_matrix(kf[...], ch, hf, 1, 2)
    w2 = conv_matrix(kf[...], ch, hf, 0, 1)
    w1c = conv_matrix(kc[...], ch, hc, 1, 2)
    w2c = conv_matrix(kc[...], ch, hc, 0, 1)
    pf = jnp.sum(jnp.where(iota((rf, hf), 1) == (iota((rf, hf), 0) & (hf - 1)), prec_f[...], 0.0), axis=1, keepdims=True)
    pc = jnp.sum(jnp.where(iota((rc, hc), 1) == (iota((rc, hc), 0) & (hc - 1)), prec_c[...], 0.0), axis=1, keepdims=True)
    to_smem.wait()

    @pl.when(jnp.logical_not(has_up))
    def _():
        halo_rx[0] = jnp.zeros(halo_rx.shape[1:], BF16)
        edge_rx[0] = jnp.zeros(edge_rx.shape[1:], F32)

    @pl.when(jnp.logical_not(has_down))
    def _():
        halo_rx[1] = jnp.zeros(halo_rx.shape[1:], BF16)
        edge_rx[1] = jnp.zeros(edge_rx.shape[1:], F32)

    def pair_wait(pairs, which):
        for side in range(2):
            @pl.when((has_up, has_down)[side])
            def _():
                if which == "recv":
                    pairs[1 - side].wait_recv()
                else:
                    pairs[side].wait_send()

    pair_wait(halo, "recv")

    q = iota((ch * (hf + 2), 1), 0)
    keep_f = jnp.logical_and(
        jnp.logical_or(has_up, jnp.logical_or(q < rf, q >= rf + ch)), jnp.logical_or(has_down, q < rf + ch)
    )
    q = iota((ch * (hc + 2), 1), 0)
    keep_c = jnp.logical_and(
        jnp.logical_or(has_up, jnp.logical_or(q < rc, q >= rc + ch)), jnp.logical_or(has_down, q < rc + ch)
    )

    def two_steps(own, above, below, force0, force1, wa, wb, keep, width):
        x = jnp.concatenate([own, above, below], axis=0)
        mixed = mm(wa, shifted(x, width))
        base = jnp.concatenate([own, above[:ch], below[:ch]], axis=0)
        y = (base + 0.5 * jnp.tanh(mixed + force0)).astype(BF16).astype(F32)
        y = jnp.where(keep, y, 0.0)
        mixed = mm(wb, shifted(y, width))
        return (y[: own.shape[0]] + 0.5 * jnp.tanh(mixed + force1)).astype(BF16)

    lane = iota((1, TILE_L), 1)
    like = jnp.zeros((1, TILE_L), F32)
    scale_f = -0.5 / math.sqrt(ch * hf * bands * lon)
    scale_c = -0.5 / math.sqrt(ch * hc * bands * lonc)

    for p in range(n_p):
        hs = [halo_rx[side, pl.ds(p * 2 * ch, 2 * ch), :].astype(F32) for side in range(2)]
        ns = [halo_rx[side, pl.ds(n_base + (p // 2) * 2 * ch, 2 * ch), :].astype(F32)[(p % 2) * ch : (p % 2 + 1) * ch]
              for side in range(2)]
        force0 = jnp.concatenate([noise[0, p].astype(F32), ns[0], ns[1]], axis=0)
        new = two_steps(fine[p].astype(F32), hs[0], hs[1], force0, noise[1, p].astype(F32), w1, w2, keep_f, lon)
        fin[p] = new
        diff = new.astype(F32) - obs_f[...].astype(F32)
        rows = jnp.sum(diff * diff, axis=1, keepdims=True)
        like = like + jnp.where(lane == p, scale_f * jnp.sum(rows * pf, axis=0, keepdims=True), 0.0)

    send1 = []
    for k in range(1, members):
        peer = lax.rem(me + k, members)
        send1.append(copy_to(tile(fin, lax.rem(peer, shares)), recv1.at[pl.ds(me * n_p, n_p)],
                             s1.at[k], r1.at[k], {"ens": peer}))
        send1[-1].start()
    own1 = pltpu.make_async_copy(tile(fin, rank), recv1.at[pl.ds(me * n_p, n_p)], loc.at[0])
    own1.start()

    pair_wait(edge, "recv")
    hs = [halo_rx[side, pl.ds(c_base, 2 * ch), :].astype(F32) for side in range(2)]
    force0 = jnp.concatenate([forcing_rows(0, 0, rc), edge_rx[0], edge_rx[1]], axis=0)
    new = two_steps(c0.astype(F32), hs[0], hs[1], force0, forcing_rows(1, 0, rc), w1c, w2c, keep_c, lonc)
    parts = []
    for p in range(n_p):
        mine = new[:, p * lonc : (p + 1) * lonc]
        parts.append(mine)
        diff = mine.astype(F32) - obs_c[...].astype(F32)
        rows = jnp.sum(diff * diff, axis=1, keepdims=True)
        like = like + jnp.where(lane == n_p + p, scale_c * jnp.sum(rows * pc, axis=0, keepdims=True), 0.0)
    likeb[band] = jnp.broadcast_to(like, likeb.shape[1:])
    send_b = []
    for k in range(1, bands):
        peer = lax.rem(band + k, bands)
        send_b.append(copy_to(likeb.at[band], likeb.at[band], bs.at[k], br.at[k], {"band": peer}))
        send_b[-1].start()

    n = n_p * rc
    lp = int(math.log2(piece))
    q = iota((n, n), 0)
    src = ((q >> lp) & (n_p - 1)) * rc + (q >> int(math.log2(n_p * piece))) * piece + (q & (piece - 1))
    cstage[...] = mm(onehot(iota((n, n), 1) == src), jnp.concatenate(parts, axis=0)).astype(BF16).reshape(cstage.shape)
    send_c = []
    for g in range(members // shares):
        for c in range(holders):
            peer = g * shares + holder(c)
            send_c.append((peer, copy_to(cstage.at[c], recvc.at[pl.ds(me * TILE_R, TILE_R)],
                                         cs1.at[g * holders + c], cr1.at[lax.rem(peer - me + members, members)],
                                         {"ens": peer})))
    for peer, desc in send_c:
        @pl.when(me != peer)
        def _():
            desc.start()

    for c in range(holders):
        @pl.when(rank == holder(c))
        def _():
            own = pltpu.make_async_copy(cstage.at[c], recvc.at[pl.ds(me * TILE_R, TILE_R)], loc.at[1])
            own.start()
            own.wait()

    own1.wait()
    for k in range(1, members):
        copy_to(tile(fin, rank), recv1.at[pl.ds(lax.rem(me - k + members, members) * n_p, n_p)],
                s1.at[k], r1.at[k], {"ens": lax.rem(me + k, members)}).wait_recv()
    send2 = []
    for k in list(range(1, shares)) + [0]:
        target = lax.rem(rank + k, shares)
        for s in range(n_p):
            slot = target * n_p + s
            chosen[slot] = recv1[par_s[0, group * n_p + slot]]
        from_ref = chosen.at[pl.ds(target * n_p, n_p)]
        if k:
            send2.append(copy_to(from_ref, tile(out_f, rank), s2.at[k], r2.at[k], {"ens": group + target}))
            send2[-1].start()
        else:
            own2 = pltpu.make_async_copy(from_ref, tile(out_f, rank), loc.at[0])
            own2.start()

    for k in range(1, bands):
        src_band = lax.rem(band - k + bands, bands)
        copy_to(likeb.at[src_band], likeb.at[src_band], bs.at[k], br.at[k],
                {"band": lax.rem(band + k, bands)}).wait_recv()
    whole = likeb[0]
    for b in range(1, bands):
        whole = whole + likeb[b]
    whole = whole[:1]
    likee[me] = whole
    send_l = []
    for k in range(1, members):
        send_l.append(copy_to(likee.at[me], likee.at[me], ls.at[k], lr.at[k], {"ens": lax.rem(me + k, members)}))
        send_l[-1].start()

    is_holder = functools.reduce(jnp.logical_or, [rank == holder(c) for c in range(holders)])
    n_slots = shares * n_p

    @pl.when(is_holder)
    def _():
        for k in range(1, members):
            copy_to(cstage.at[0], recvc.at[pl.ds(lax.rem(me - k + members, members) * TILE_R, TILE_R)],
                    cs1.at[0], cr1.at[k], {"ens": lax.rem(me + k, members)}).wait_recv()
        want = group * n_p + (iota((n_slots * piece, total), 0) >> lp)
        who = jnp.sum(jnp.where(dest[...] == want, parent, 0), axis=1, keepdims=True)
        inner = iota((n_slots * piece, 1), 0) & (piece - 1)
        pick = onehot(iota((n_slots * piece, total * piece), 1) == who * piece + inner)
        cchosen[...] = mm(pick, recvc[...]).astype(BF16).reshape(cchosen.shape)

    for c in range(holders):
        @pl.when(rank == holder(c))
        def _():
            for k in range(1, shares):
                target = lax.rem(rank + k, shares)
                copy_to(cchosen.at[target], recvc2.at[pl.ds(c * TILE_R, TILE_R)], cs2.at[k], cr2.at[c],
                        {"ens": group + target}).start()
            own = pltpu.make_async_copy(cchosen.at[rank], recvc2.at[pl.ds(c * TILE_R, TILE_R)], loc.at[1])
            own.start()
            own.wait()

    for k in range(1, members):
        src_m = lax.rem(me - k + members, members)
        copy_to(likee.at[src_m], likee.at[src_m], ls.at[k], lr.at[k], {"ens": lax.rem(me + k, members)}).wait_recv()
    everyone = likee[...].reshape(members, TILE_L)
    lane_all = iota((members, TILE_L), 1)
    for first, out in ((0, out_lf), (n_p, out_lc)):
        here = jnp.logical_and(lane_all >= first, lane_all < first + n_p)
        vals = jnp.where(here, everyone, -jnp.inf)
        peak = jnp.max(jnp.max(vals, axis=1, keepdims=True), axis=0, keepdims=True)
        part = jnp.where(here, jnp.exp(vals - peak), 0.0)
        norm = jnp.sum(jnp.sum(part, axis=1, keepdims=True), axis=0, keepdims=True)
        out[...] = (whole - (peak + jnp.log(norm)))[:, first : first + n_p]

    for c in range(holders):
        @pl.when(rank != holder(c))
        def _():
            copy_to(cchosen.at[0], recvc2.at[pl.ds(c * TILE_R, TILE_R)], cs2.at[0], cr2.at[c],
                    {"ens": group + holder(c)}).wait_recv()
    q = iota((n, n), 0)
    row = q & (rc - 1)
    src = (row >> lp) * (n_p * piece) + (q >> int(math.log2(rc))) * piece + (row & (piece - 1))
    out_c[...] = mm(onehot(iota((n, n), 1) == src), recvc2[...]).astype(BF16)

    own2.wait()
    for k in range(1, shares):
        source = lax.rem(rank - k + shares, shares)
        copy_to(chosen.at[pl.ds(0, n_p)], tile(out_f, source), s2.at[k], r2.at[k],
                {"ens": group + lax.rem(rank + k, shares)}).wait_recv()

    pair_wait(halo, "send")
    pair_wait(edge, "send")
    for desc in send1 + send2 + send_b + send_l:
        desc.wait_send()
    for peer, desc in send_c:
        @pl.when(me != peer)
        def _():
            desc.wait_send()

    @pl.when(is_holder)
    def _():
        for k in range(1, shares):
            copy_to(cchosen.at[0], recvc2.at[pl.ds(0, TILE_R)], cs2.at[k], cr2.at[0],
                    {"ens": group + lax.rem(rank + k, shares)}).wait_send()


def shards(fine, coarse, noise, kf, kc, obs_f, obs_c, prec_f, prec_c, offspring, dest_slot):
    bands, members = lax.axis_size("band"), lax.axis_size("ens")
    n_p, ch, hf, lon = fine.shape
    hc, lonc = coarse.shape[2:]
    rf, rc = ch * hf, ch * hc
    total = offspring.shape[0]
    shares = (rf // TILE_R) * (lon // TILE_L)
    holders = n_p * rc // TILE_R
    groups = members // shares
    lane_w = -(-total // TILE_L) * TILE_L
    halo_rows = n_p * 3 * ch + 2 * ch
    dma = pltpu.SemaphoreType.DMA
    vmem = pl.BlockSpec(memory_space=pltpu.VMEM)
    of, oc, lf, lc = pl.pallas_call(
        functools.partial(kernel, bands, members),
        out_shape=(
            jax.ShapeDtypeStruct((n_p, rf, lon), BF16),
            jax.ShapeDtypeStruct((n_p * rc, lonc), BF16),
            jax.ShapeDtypeStruct((1, n_p), F32),
            jax.ShapeDtypeStruct((1, n_p), F32),
        ),
        in_specs=[vmem] * 11,
        out_specs=(vmem,) * 4,
        scratch_shapes=[
            pltpu.VMEM((2, halo_rows, lon), BF16),
            pltpu.VMEM((2, halo_rows, lon), BF16),
            pltpu.VMEM((2, ch, n_p * lonc), F32),
            pltpu.VMEM((2, ch, n_p * lonc), F32),
            pltpu.VMEM((n_p, rf, lon), BF16),
            pltpu.VMEM((total, TILE_R, TILE_L), BF16),
            pltpu.VMEM((shares * n_p, TILE_R, TILE_L), BF16),
            pltpu.VMEM((holders, TILE_R, TILE_L), BF16),
            pltpu.VMEM((members * TILE_R, TILE_L), BF16),
            pltpu.VMEM((shares, TILE_R, TILE_L), BF16),
            pltpu.VMEM((holders * TILE_R, TILE_L), BF16),
            pltpu.VMEM((bands, 8, TILE_L), F32),
            pltpu.VMEM((members, 1, TILE_L), F32),
            pltpu.VMEM((1, lane_w), I32),
            pltpu.SMEM((1, lane_w), I32),
            dma((2,)), dma((2,)), dma((2,)), dma((2,)),
            dma((members,)), dma((members,)), dma((shares,)), dma((shares,)),
            dma((groups * holders,)), dma((members,)), dma((shares,)), dma((holders,)),
            dma((bands,)), dma((bands,)), dma((members,)), dma((members,)), dma((2,)),
        ],
        compiler_params=pltpu.CompilerParams(
            collective_id=0, has_side_effects=True, vmem_limit_bytes=40 * 1024 * 1024
        ),
    )(
        fine.reshape(n_p, rf, lon),
        coarse.reshape(n_p * rc, lonc),
        noise.reshape(2, n_p, rf, lon),
        kf, kc,
        obs_f.reshape(rf, lon),
        obs_c.reshape(rc, lonc),
        prec_f.reshape(1, hf),
        prec_c.reshape(1, hc),
        offspring.reshape(1, total),
        dest_slot.reshape(1, total),
    )
    return (
        of.reshape(n_p, ch, hf, lon),
        oc.reshape(n_p, ch, hc, lonc),
        lf.reshape(n_p),
        lc.reshape(n_p),
    )


def solution(mesh):
    return jax.shard_map(
        shards,
        mesh=mesh,
        in_specs=(
            P("ens", None, "band", None),
            P("ens", None, "band", None),
            P(None, "ens", None, "band", None),
            P(),
            P(),
            P(None, "band", None),
            P(None, "band", None),
            P("band"),
            P("band"),
            P(),
            P(),
        ),
        out_specs=(P("ens", None, "band", None), P("ens", None, "band", None), P("ens"), P("ens")),
        check_vma=False,
    )
```

```python
import functools
import math

import jax
import jax.numpy as jnp
from jax import lax
from jax.experimental import pallas as pl
from jax.experimental.pallas import tpu as pltpu
from jax.sharding import PartitionSpec as P

F32 = jnp.float32
BF16 = jnp.bfloat16
I32 = jnp.int32
TILE_R = 16
TILE_L = 128
VMEM_LIMIT = 56 * 1024 * 1024


def iota(shape, dim):
    return lax.broadcasted_iota(I32, shape, dim)


def onehot(cond):
    return jnp.where(cond, 1.0, 0.0).astype(BF16)


def mm(a, b):
    return jnp.dot(a, b, preferred_element_type=F32)


def layout(idx, ch, rows, halo):
    base = ch * rows
    own_c, own_r = idx >> int(math.log2(rows)), idx & (rows - 1)
    if halo == 0:
        return own_c, own_r
    up = idx - base
    down = up - halo * ch
    above = -1 - jnp.where(up >= ch, 1, 0)
    below = rows + jnp.where(down >= ch, 1, 0)
    side_c = up & (ch - 1)
    side_r = jnp.where(down < 0, above, below)
    return jnp.where(idx < base, own_c, side_c), jnp.where(idx < base, own_r, side_r)


def conv_matrix(kern, ch, rows, halo_out, halo_in):
    n_out = ch * (rows + 2 * halo_out)
    n_in = ch * (rows + 2 * halo_in)
    o, r_out = layout(iota((n_out, 1), 0), ch, rows, halo_out)
    col = iota((1, 3 * n_in), 1)
    shift = jnp.where(col >= n_in, 1, 0) + jnp.where(col >= 2 * n_in, 1, 0)
    i, r_in = layout(col - n_in * shift, ch, rows, halo_in)
    spread = mm(onehot(o == iota((n_out, ch), 1)), kern).astype(BF16)
    taps = iota((9 * ch, 3 * n_in), 0)
    total = None
    for a in range(3):
        pick = mm(spread, onehot(taps == 9 * i + 3 * a + shift))
        term = jnp.where(r_in - r_out + 1 == a, pick, 0.0)
        total = term if total is None else total + term
    return total.astype(BF16)


def shifted(x, width):
    parts = [x[:, j : j + width] for j in range(0, x.shape[1], width)]
    left = [pltpu.roll(v, 1, 1) for v in parts]
    right = [pltpu.roll(v, width - 1, 1) for v in parts]
    join = lambda vs: vs[0] if len(vs) == 1 else jnp.concatenate(vs, axis=1)
    return jnp.concatenate([join(left), x, join(right)], axis=0).astype(BF16)


def kernel(
    bands, members,
    fine_h, coarse_h, noise_h, kf_h, kc_h, obs_f_h, obs_c_h, prec_f_h, prec_c_h, offs_h, dest_h,
    out_f, out_c, out_lf, out_lc,
    fine, coarse, noise, kf, kc, obs_f, obs_c, prec_f, prec_c, offs, dest, in_sem,
    halo_tx, halo_rx, edge_tx, edge_rx, fin, recv1, chosen, cstage, recvc, cchosen, recvc2,
    likeb, likee, par_v, par_s,
    h_send, h_recv, e_send, e_recv, s1, r1, s2, r2, cs1, cr1, cs2, cr2, bs, br, ls, lr, loc,
):
    band = lax.axis_index("band")
    me = lax.axis_index("ens")
    n_p, ch, hf, lon = fine.shape[0], kf.shape[0], prec_f.shape[1], fine.shape[2]
    hc, lonc = prec_c.shape[1], coarse.shape[1]
    rf, rc = ch * hf, ch * hc
    lane_blocks = lon // TILE_L
    shares = (rf // TILE_R) * lane_blocks
    holders = n_p * rc // TILE_R
    piece = rc // holders
    total = offs.shape[1]
    group = (me // shares) * shares
    rank = me - group

    def holder(c):
        return c * (shares // holders) + (c % 2) * (shares // holders // 2)

    def tile(ref, share):
        row = pl.multiple_of((share // lane_blocks) * TILE_R, TILE_R)
        lane = pl.multiple_of((share % lane_blocks) * TILE_L, TILE_L)
        return ref.at[:, pl.ds(row, TILE_R), pl.ds(lane, TILE_L)]

    def copy_to(src, dst, send, recv, device):
        return pltpu.make_async_remote_copy(
            src_ref=src, dst_ref=dst, send_sem=send, recv_sem=recv,
            device_id=device, device_id_type=pl.DeviceIdType.MESH,
        )

    sources = (fine_h, noise_h, coarse_h, kf_h, kc_h, obs_f_h, obs_c_h, prec_f_h, prec_c_h, offs_h, dest_h)
    places = (fine, noise, coarse, kf, kc, obs_f, obs_c, prec_f, prec_c, offs, dest)
    loads = [pltpu.make_async_copy(a, b, in_sem.at[i]) for i, (a, b) in enumerate(zip(sources, places))]
    for load in loads:
        load.start()

    barrier = pltpu.get_barrier_semaphore()
    for k in range(1, members):
        pl.semaphore_signal(barrier, inc=1, device_id={"ens": lax.rem(me + k, members)},
                            device_id_type=pl.DeviceIdType.MESH)
    for k in range(1, bands):
        pl.semaphore_signal(barrier, inc=1, device_id={"band": lax.rem(band + k, bands)},
                            device_id_type=pl.DeviceIdType.MESH)

    def edge_rows(n_side, rows):
        q = iota((2 * n_side, ch * rows), 0)
        lower = q >= n_side
        t = jnp.where(lower, q - n_side, q)
        depth = jnp.where(t >= ch, 1, 0)
        row = jnp.where(lower, rows - 1 - depth, depth)
        return onehot(iota((2 * n_side, ch * rows), 1) == (t & (ch - 1)) * rows + row)

    sel_state, sel_noise, sel_coarse = edge_rows(2 * ch, hf), edge_rows(ch, hf), edge_rows(2 * ch, hc)
    n_base = n_p * 2 * ch
    c_base = n_base + n_p * ch
    picked_noise = []
    for load in loads[:3]:
        load.wait()
    for p in range(n_p):
        rows = mm(sel_state, fine[p]).astype(BF16)
        halo_tx[0, pl.ds(p * 2 * ch, 2 * ch), :] = rows[: 2 * ch]
        halo_tx[1, pl.ds(p * 2 * ch, 2 * ch), :] = rows[2 * ch :]
        picked_noise.append(mm(sel_noise, noise[0, p]))
    for side in range(2):
        halo_tx[side, pl.ds(n_base, n_p * ch), :] = jnp.concatenate(
            [v[side * ch : (side + 1) * ch] for v in picked_noise], axis=0
        ).astype(BF16)
    c0 = jnp.concatenate([coarse[pl.ds(p * rc, rc), :] for p in range(n_p)], axis=1)
    rows = mm(sel_coarse, c0).astype(BF16)
    halo_tx[0, pl.ds(c_base, 2 * ch), :] = rows[: 2 * ch]
    halo_tx[1, pl.ds(c_base, 2 * ch), :] = rows[2 * ch :]

    pl.semaphore_wait(barrier, members + bands - 2)

    up, down = lax.max(band - 1, 0), lax.min(band + 1, bands - 1)
    has_up, has_down = band > 0, band < bands - 1

    def pair(tx, rx, send, recv, side):
        return copy_to(tx.at[side], rx.at[1 - side], send.at[side], recv.at[1 - side],
                       {"band": up if side == 0 else down})

    halo = [pair(halo_tx, halo_rx, h_send, h_recv, side) for side in range(2)]
    edge = [pair(edge_tx, edge_rx, e_send, e_recv, side) for side in range(2)]

    @pl.when(has_up)
    def _():
        halo[0].start()

    @pl.when(has_down)
    def _():
        halo[1].start()

    r4 = hf // hc
    q = iota((rc + 2 * ch, rf), 0)
    cell_c = jnp.where(q < rc, q >> int(math.log2(hc)), (q - rc) & (ch - 1))
    cell_r = jnp.where(q < rc, q & (hc - 1), jnp.where(q < rc + ch, 0, hc - 1))
    src = iota((rc + 2 * ch, rf), 1)
    gather_rows = onehot((src >> int(math.log2(r4))) == cell_c * hc + cell_r)
    l4 = lon // lonc
    fold = onehot((iota((lon, lonc), 0) >> int(math.log2(l4))) == iota((lon, lonc), 1))
    sums = jnp.concatenate(
        [mm(gather_rows, noise[s, p]) for s in range(2) for p in range(n_p)], axis=0
    )
    hi = sums.astype(BF16)
    rest = sums - hi.astype(F32)
    mid = rest.astype(BF16)
    low = (rest - mid.astype(F32)).astype(BF16)
    scale_r = 4.0 / (r4 * l4)
    folded = (mm(hi, fold) + (mm(mid, fold) + mm(low, fold))) * scale_r
    block = rc + 2 * ch

    def forcing_rows(step, lo, n):
        return jnp.concatenate(
            [folded[(step * n_p + p) * block + lo : (step * n_p + p) * block + lo + n] for p in range(n_p)],
            axis=1,
        )

    edge_tx[0] = forcing_rows(0, rc, ch)
    edge_tx[1] = forcing_rows(0, rc + ch, ch)

    @pl.when(has_up)
    def _():
        edge[0].start()

    @pl.when(has_down)
    def _():
        edge[1].start()

    for load in loads[3:]:
        load.wait()
    lane_w = par_v.shape[1]
    lanes = iota((total, total), 1)
    subs = iota((total, total), 0)
    ends = jnp.sum(jnp.where(lanes <= subs, offs[...], 0), axis=1, keepdims=True)
    parent = jnp.sum(jnp.where(ends <= lanes, 1, 0), axis=0, keepdims=True)
    slot_col = jnp.sum(jnp.where(dest[...] == subs, parent, 0), axis=1, keepdims=True)
    par_v[...] = jnp.sum(
        jnp.where(iota((total, lane_w), 0) == iota((total, lane_w), 1), jnp.minimum(slot_col, total - 1), 0),
        axis=0, keepdims=True,
    )
    to_smem = pltpu.make_async_copy(par_v, par_s, loc.at[0])
    to_smem.start()

    w1 = conv_matrix(kf[...], ch, hf, 1, 2)
    w2 = conv_matrix(kf[...], ch, hf, 0, 1)
    w1c = conv_matrix(kc[...], ch, hc, 1, 2)
    w2c = conv_matrix(kc[...], ch, hc, 0, 1)
    pf = jnp.sum(jnp.where(iota((rf, hf), 1) == (iota((rf, hf), 0) & (hf - 1)), prec_f[...], 0.0), axis=1, keepdims=True)
    pc = jnp.sum(jnp.where(iota((rc, hc), 1) == (iota((rc, hc), 0) & (hc - 1)), prec_c[...], 0.0), axis=1, keepdims=True)
    to_smem.wait()

    @pl.when(jnp.logical_not(has_up))
    def _():
        halo_rx[0] = jnp.zeros(halo_rx.shape[1:], BF16)
        edge_rx[0] = jnp.zeros(edge_rx.shape[1:], F32)

    @pl.when(jnp.logical_not(has_down))
    def _():
        halo_rx[1] = jnp.zeros(halo_rx.shape[1:], BF16)
        edge_rx[1] = jnp.zeros(edge_rx.shape[1:], F32)

    def pair_wait(pairs, which):
        for side in range(2):
            @pl.when((has_up, has_down)[side])
            def _():
                if which == "recv":
                    pairs[1 - side].wait_recv()
                else:
                    pairs[side].wait_send()

    pair_wait(halo, "recv")

    q = iota((ch * (hf + 2), 1), 0)
    keep_f = jnp.logical_and(
        jnp.logical_or(has_up, jnp.logical_or(q < rf, q >= rf + ch)), jnp.logical_or(has_down, q < rf + ch)
    )
    q = iota((ch * (hc + 2), 1), 0)
    keep_c = jnp.logical_and(
        jnp.logical_or(has_up, jnp.logical_or(q < rc, q >= rc + ch)), jnp.logical_or(has_down, q < rc + ch)
    )

    def two_steps(own, above, below, force0, force1, wa, wb, keep, width):
        x = jnp.concatenate([own, above, below], axis=0)
        mixed = mm(wa, shifted(x, width))
        base = jnp.concatenate([own, above[:ch], below[:ch]], axis=0)
        y = (base + 0.5 * jnp.tanh(mixed + force0)).astype(BF16).astype(F32)
        y = jnp.where(keep, y, 0.0)
        mixed = mm(wb, shifted(y, width))
        return (y[: own.shape[0]] + 0.5 * jnp.tanh(mixed + force1)).astype(BF16)

    lane = iota((1, TILE_L), 1)
    like = jnp.zeros((1, TILE_L), F32)
    scale_f = -0.5 / math.sqrt(ch * hf * bands * lon)
    scale_c = -0.5 / math.sqrt(ch * hc * bands * lonc)

    send1, own1 = [], []
    batch = n_p // 2
    part1 = lambda ref, first, b: ref.at[pl.ds(first * n_p + b * batch, batch)]

    def share1(share, b):
        row = pl.multiple_of((share // lane_blocks) * TILE_R, TILE_R)
        at = pl.multiple_of((share % lane_blocks) * TILE_L, TILE_L)
        return fin.at[pl.ds(b * batch, batch), pl.ds(row, TILE_R), pl.ds(at, TILE_L)]

    for p in range(n_p):
        hs = [halo_rx[side, pl.ds(p * 2 * ch, 2 * ch), :].astype(F32) for side in range(2)]
        ns = [halo_rx[side, pl.ds(n_base + (p // 2) * 2 * ch, 2 * ch), :].astype(F32)[(p % 2) * ch : (p % 2 + 1) * ch]
              for side in range(2)]
        force0 = jnp.concatenate([noise[0, p].astype(F32), ns[0], ns[1]], axis=0)
        new = two_steps(fine[p].astype(F32), hs[0], hs[1], force0, noise[1, p].astype(F32), w1, w2, keep_f, lon)
        fin[p] = new
        diff = new.astype(F32) - obs_f[...].astype(F32)
        rows = jnp.sum(diff * diff, axis=1, keepdims=True)
        like = like + jnp.where(lane == p, scale_f * jnp.sum(rows * pf, axis=0, keepdims=True), 0.0)

        if (p + 1) % batch == 0:
            b = p // batch
            for k in range(1, members):
                peer = lax.rem(me + k, members)
                send1.append(copy_to(share1(lax.rem(peer, shares), b), part1(recv1, me, b),
                                     s1.at[b * members + k], r1.at[b * members + k], {"ens": peer}))
                send1[-1].start()
            own1.append(pltpu.make_async_copy(share1(rank, b), part1(recv1, me, b), loc.at[2 + b]))
            own1[-1].start()

    pair_wait(edge, "recv")
    hs = [halo_rx[side, pl.ds(c_base, 2 * ch), :].astype(F32) for side in range(2)]
    force0 = jnp.concatenate([forcing_rows(0, 0, rc), edge_rx[0], edge_rx[1]], axis=0)
    new = two_steps(c0.astype(F32), hs[0], hs[1], force0, forcing_rows(1, 0, rc), w1c, w2c, keep_c, lonc)
    parts = []
    for p in range(n_p):
        mine = new[:, p * lonc : (p + 1) * lonc]
        parts.append(mine)
        diff = mine.astype(F32) - obs_c[...].astype(F32)
        rows = jnp.sum(diff * diff, axis=1, keepdims=True)
        like = like + jnp.where(lane == n_p + p, scale_c * jnp.sum(rows * pc, axis=0, keepdims=True), 0.0)
    likeb[band] = jnp.broadcast_to(like, likeb.shape[1:])
    send_b = []
    for k in range(1, bands):
        peer = lax.rem(band + k, bands)
        send_b.append(copy_to(likeb.at[band], likeb.at[band], bs.at[k], br.at[k], {"band": peer}))
        send_b[-1].start()

    n = n_p * rc
    lp = int(math.log2(piece))
    q = iota((n, n), 0)
    src = ((q >> lp) & (n_p - 1)) * rc + (q >> int(math.log2(n_p * piece))) * piece + (q & (piece - 1))
    cstage[...] = mm(onehot(iota((n, n), 1) == src), jnp.concatenate(parts, axis=0)).astype(BF16).reshape(cstage.shape)
    send_c = []
    for g in range(members // shares):
        for c in range(holders):
            peer = g * shares + holder(c)
            send_c.append((peer, copy_to(cstage.at[c], recvc.at[pl.ds(me * TILE_R, TILE_R)],
                                         cs1.at[g * holders + c], cr1.at[lax.rem(peer - me + members, members)],
                                         {"ens": peer})))
    for peer, desc in send_c:
        @pl.when(me != peer)
        def _():
            desc.start()

    for c in range(holders):
        @pl.when(rank == holder(c))
        def _():
            own = pltpu.make_async_copy(cstage.at[c], recvc.at[pl.ds(me * TILE_R, TILE_R)], loc.at[1])
            own.start()
            own.wait()

    for b in range(2):
        own1[b].wait()
        for k in range(1, members):
            copy_to(share1(rank, b), part1(recv1, lax.rem(me - k + members, members), b),
                    s1.at[b * members + k], r1.at[b * members + k],
                    {"ens": lax.rem(me + k, members)}).wait_recv()
    send2 = []
    for k in list(range(1, shares)) + [0]:
        target = lax.rem(rank + k, shares)
        for s in range(n_p):
            slot = target * n_p + s
            chosen[slot] = recv1[par_s[0, group * n_p + slot]]
        from_ref = chosen.at[pl.ds(target * n_p, n_p)]
        if k:
            send2.append(copy_to(from_ref, tile(out_f, rank), s2.at[k], r2.at[k], {"ens": group + target}))
            send2[-1].start()
        else:
            own2 = pltpu.make_async_copy(from_ref, tile(out_f, rank), loc.at[0])
            own2.start()

    for k in range(1, bands):
        src_band = lax.rem(band - k + bands, bands)
        copy_to(likeb.at[src_band], likeb.at[src_band], bs.at[k], br.at[k],
                {"band": lax.rem(band + k, bands)}).wait_recv()
    whole = likeb[0]
    for b in range(1, bands):
        whole = whole + likeb[b]
    whole = whole[:1]
    likee[me] = whole
    send_l = []
    for k in range(1, members):
        send_l.append(copy_to(likee.at[me], likee.at[me], ls.at[k], lr.at[k], {"ens": lax.rem(me + k, members)}))
        send_l[-1].start()

    is_holder = functools.reduce(jnp.logical_or, [rank == holder(c) for c in range(holders)])
    n_slots = shares * n_p

    @pl.when(is_holder)
    def _():
        for k in range(1, members):
            copy_to(cstage.at[0], recvc.at[pl.ds(lax.rem(me - k + members, members) * TILE_R, TILE_R)],
                    cs1.at[0], cr1.at[k], {"ens": lax.rem(me + k, members)}).wait_recv()
        want = group * n_p + (iota((n_slots * piece, total), 0) >> lp)
        who = jnp.sum(jnp.where(dest[...] == want, parent, 0), axis=1, keepdims=True)
        inner = iota((n_slots * piece, 1), 0) & (piece - 1)
        pick = onehot(iota((n_slots * piece, total * piece), 1) == who * piece + inner)
        cchosen[...] = mm(pick, recvc[...]).astype(BF16).reshape(cchosen.shape)

    for c in range(holders):
        @pl.when(rank == holder(c))
        def _():
            for k in range(1, shares):
                target = lax.rem(rank + k, shares)
                copy_to(cchosen.at[target], recvc2.at[pl.ds(c * TILE_R, TILE_R)], cs2.at[k], cr2.at[c],
                        {"ens": group + target}).start()
            own = pltpu.make_async_copy(cchosen.at[rank], recvc2.at[pl.ds(c * TILE_R, TILE_R)], loc.at[1])
            own.start()
            own.wait()

    for k in range(1, members):
        src_m = lax.rem(me - k + members, members)
        copy_to(likee.at[src_m], likee.at[src_m], ls.at[k], lr.at[k], {"ens": lax.rem(me + k, members)}).wait_recv()
    everyone = likee[...].reshape(members, TILE_L)
    lane_all = iota((members, TILE_L), 1)
    for first, out in ((0, out_lf), (n_p, out_lc)):
        here = jnp.logical_and(lane_all >= first, lane_all < first + n_p)
        vals = jnp.where(here, everyone, -jnp.inf)
        peak = jnp.max(jnp.max(vals, axis=1, keepdims=True), axis=0, keepdims=True)
        part = jnp.where(here, jnp.exp(vals - peak), 0.0)
        norm = jnp.sum(jnp.sum(part, axis=1, keepdims=True), axis=0, keepdims=True)
        out[...] = (whole - (peak + jnp.log(norm)))[:, first : first + n_p]

    for c in range(holders):
        @pl.when(rank != holder(c))
        def _():
            copy_to(cchosen.at[0], recvc2.at[pl.ds(c * TILE_R, TILE_R)], cs2.at[0], cr2.at[c],
                    {"ens": group + holder(c)}).wait_recv()
    q = iota((n, n), 0)
    row = q & (rc - 1)
    src = (row >> lp) * (n_p * piece) + (q >> int(math.log2(rc))) * piece + (row & (piece - 1))
    out_c[...] = mm(onehot(iota((n, n), 1) == src), recvc2[...]).astype(BF16)

    own2.wait()
    for k in range(1, shares):
        source = lax.rem(rank - k + shares, shares)
        copy_to(chosen.at[pl.ds(0, n_p)], tile(out_f, source), s2.at[k], r2.at[k],
                {"ens": group + lax.rem(rank + k, shares)}).wait_recv()

    pair_wait(halo, "send")
    pair_wait(edge, "send")
    for desc in send1 + send2 + send_b + send_l:
        desc.wait_send()
    for peer, desc in send_c:
        @pl.when(me != peer)
        def _():
            desc.wait_send()

    @pl.when(is_holder)
    def _():
        for k in range(1, shares):
            copy_to(cchosen.at[0], recvc2.at[pl.ds(0, TILE_R)], cs2.at[k], cr2.at[0],
                    {"ens": group + lax.rem(rank + k, shares)}).wait_send()


def write_out(*refs):
    count = (len(refs) - 1) // 2
    copies = [pltpu.make_async_copy(refs[i], refs[count + i], refs[-1].at[i]) for i in range(count)]
    for copy in copies:
        copy.start()
    for copy in copies:
        copy.wait()


def shards(fine, coarse, noise, kf, kc, obs_f, obs_c, prec_f, prec_c, offspring, dest_slot):
    bands, members = lax.axis_size("band"), lax.axis_size("ens")
    n_p, ch, hf, lon = fine.shape
    hc, lonc = coarse.shape[2:]
    rf, rc = ch * hf, ch * hc
    total = offspring.shape[0]
    shares = (rf // TILE_R) * (lon // TILE_L)
    holders = n_p * rc // TILE_R
    groups = members // shares
    lane_w = -(-total // TILE_L) * TILE_L
    halo_rows = n_p * 3 * ch + 2 * ch
    dma = pltpu.SemaphoreType.DMA
    vmem = pl.BlockSpec(memory_space=pltpu.VMEM)
    hbm = pl.BlockSpec(memory_space=pl.ANY)
    args = (
        fine.reshape(n_p, rf, lon),
        coarse.reshape(n_p * rc, lonc),
        noise.reshape(2, n_p, rf, lon),
        kf, kc,
        obs_f.reshape(rf, lon),
        obs_c.reshape(rc, lonc),
        prec_f.reshape(1, hf),
        prec_c.reshape(1, hc),
        offspring.reshape(1, total),
        dest_slot.reshape(1, total),
    )
    results = (
        jax.ShapeDtypeStruct((n_p, rf, lon), BF16),
        jax.ShapeDtypeStruct((n_p * rc, lonc), BF16),
        jax.ShapeDtypeStruct((1, n_p), F32),
        jax.ShapeDtypeStruct((1, n_p), F32),
    )
    done = pl.pallas_call(
        functools.partial(kernel, bands, members),
        out_shape=results,
        in_specs=[hbm] * 11,
        out_specs=(vmem,) * 4,
        scratch_shapes=[pltpu.VMEM(a.shape, a.dtype) for a in args] + [
            dma((11,)),
            pltpu.VMEM((2, halo_rows, lon), BF16),
            pltpu.VMEM((2, halo_rows, lon), BF16),
            pltpu.VMEM((2, ch, n_p * lonc), F32),
            pltpu.VMEM((2, ch, n_p * lonc), F32),
            pltpu.VMEM((n_p, rf, lon), BF16),
            pltpu.VMEM((total, TILE_R, TILE_L), BF16),
            pltpu.VMEM((shares * n_p, TILE_R, TILE_L), BF16),
            pltpu.VMEM((holders, TILE_R, TILE_L), BF16),
            pltpu.VMEM((members * TILE_R, TILE_L), BF16),
            pltpu.VMEM((shares, TILE_R, TILE_L), BF16),
            pltpu.VMEM((holders * TILE_R, TILE_L), BF16),
            pltpu.VMEM((bands, 8, TILE_L), F32),
            pltpu.VMEM((members, 1, TILE_L), F32),
            pltpu.VMEM((1, lane_w), I32),
            pltpu.SMEM((1, lane_w), I32),
            dma((2,)), dma((2,)), dma((2,)), dma((2,)),
            dma((2 * members,)), dma((2 * members,)), dma((shares,)), dma((shares,)),
            dma((groups * holders,)), dma((members,)), dma((shares,)), dma((holders,)),
            dma((bands,)), dma((bands,)), dma((members,)), dma((members,)), dma((4,)),
        ],
        compiler_params=pltpu.CompilerParams(
            collective_id=0, has_side_effects=True, vmem_limit_bytes=VMEM_LIMIT
        ),
    )(*args)
    of, oc, lf, lc = pl.pallas_call(
        write_out,
        out_shape=results,
        in_specs=[hbm] * 4,
        out_specs=(hbm,) * 4,
        scratch_shapes=[dma((4,))],
    )(*done)
    return (
        of.reshape(n_p, ch, hf, lon),
        oc.reshape(n_p, ch, hc, lonc),
        lf.reshape(n_p),
        lc.reshape(n_p),
    )


def solution(mesh):
    return jax.shard_map(
        shards,
        mesh=mesh,
        in_specs=(
            P("ens", None, "band", None),
            P("ens", None, "band", None),
            P(None, "ens", None, "band", None),
            P(),
            P(),
            P(None, "band", None),
            P(None, "band", None),
            P("band"),
            P("band"),
            P(),
            P(),
        ),
        out_specs=(P("ens", None, "band", None), P("ens", None, "band", None), P("ens"), P("ens")),
        check_vma=False,
    )
```

```python
import functools
import math

import jax
import jax.numpy as jnp
from jax import lax
from jax.experimental import pallas as pl
from jax.experimental.pallas import tpu as pltpu
from jax.sharding import PartitionSpec as P

F32 = jnp.float32
BF16 = jnp.bfloat16
I32 = jnp.int32
TILE_R = 16
TILE_L = 128
VMEM_LIMIT = 56 * 1024 * 1024


def iota(shape, dim):
    return lax.broadcasted_iota(I32, shape, dim)


def onehot(cond):
    return jnp.where(cond, 1.0, 0.0).astype(BF16)


def mm(a, b):
    return jnp.dot(a, b, preferred_element_type=F32)


def layout(idx, ch, rows, halo):
    base = ch * rows
    own_c, own_r = idx >> int(math.log2(rows)), idx & (rows - 1)
    if halo == 0:
        return own_c, own_r
    up = idx - base
    down = up - halo * ch
    above = -1 - jnp.where(up >= ch, 1, 0)
    below = rows + jnp.where(down >= ch, 1, 0)
    side_c = up & (ch - 1)
    side_r = jnp.where(down < 0, above, below)
    return jnp.where(idx < base, own_c, side_c), jnp.where(idx < base, own_r, side_r)


def conv_matrix(kern, ch, rows, halo_out, halo_in):
    n_out = ch * (rows + 2 * halo_out)
    n_in = ch * (rows + 2 * halo_in)
    o, r_out = layout(iota((n_out, 1), 0), ch, rows, halo_out)
    col = iota((1, 3 * n_in), 1)
    shift = jnp.where(col >= n_in, 1, 0) + jnp.where(col >= 2 * n_in, 1, 0)
    i, r_in = layout(col - n_in * shift, ch, rows, halo_in)
    spread = mm(onehot(o == iota((n_out, ch), 1)), kern).astype(BF16)
    taps = iota((9 * ch, 3 * n_in), 0)
    total = None
    for a in range(3):
        pick = mm(spread, onehot(taps == 9 * i + 3 * a + shift))
        term = jnp.where(r_in - r_out + 1 == a, pick, 0.0)
        total = term if total is None else total + term
    return total.astype(BF16)


def shifted(x, width):
    parts = [x[:, j : j + width] for j in range(0, x.shape[1], width)]
    left = [pltpu.roll(v, 1, 1) for v in parts]
    right = [pltpu.roll(v, width - 1, 1) for v in parts]
    join = lambda vs: vs[0] if len(vs) == 1 else jnp.concatenate(vs, axis=1)
    return jnp.concatenate([join(left), x, join(right)], axis=0).astype(BF16)


def kernel(
    bands, members,
    fine_h, coarse_h, noise_h, kf_h, kc_h, obs_f_h, obs_c_h, prec_f_h, prec_c_h, offs_h, dest_h,
    out_f, out_c, out_lf, out_lc,
    fine, coarse, noise, kf, kc, obs_f, obs_c, prec_f, prec_c, offs, dest, in_sem,
    halo_tx, halo_rx, edge_tx, edge_rx, fin, recv1, chosen, cstage, recvc, cchosen, recvc2,
    likeb, likee, par_v, par_s,
    h_send, h_recv, e_send, e_recv, s1, r1, s2, r2, cs1, cr1, cs2, cr2, bs, br, ls, lr, loc,
):
    band = lax.axis_index("band")
    me = lax.axis_index("ens")
    n_p, ch, hf, lon = fine.shape[0], kf.shape[0], prec_f.shape[1], fine.shape[2]
    hc, lonc = prec_c.shape[1], coarse.shape[1]
    rf, rc = ch * hf, ch * hc
    lane_blocks = lon // TILE_L
    shares = (rf // TILE_R) * lane_blocks
    holders = n_p * rc // TILE_R
    piece = rc // holders
    total = offs.shape[1]
    group = (me // shares) * shares
    rank = me - group

    def holder(c):
        return c * (shares // holders) + (c % 2) * (shares // holders // 2)

    def tile(ref, share):
        row = pl.multiple_of((share // lane_blocks) * TILE_R, TILE_R)
        lane = pl.multiple_of((share % lane_blocks) * TILE_L, TILE_L)
        return ref.at[:, pl.ds(row, TILE_R), pl.ds(lane, TILE_L)]

    def copy_to(src, dst, send, recv, device):
        return pltpu.make_async_remote_copy(
            src_ref=src, dst_ref=dst, send_sem=send, recv_sem=recv,
            device_id=device, device_id_type=pl.DeviceIdType.MESH,
        )

    sources = (fine_h, noise_h, coarse_h, kf_h, kc_h, obs_f_h, obs_c_h, prec_f_h, prec_c_h, offs_h, dest_h)
    places = (fine, noise, coarse, kf, kc, obs_f, obs_c, prec_f, prec_c, offs, dest)
    loads = [pltpu.make_async_copy(a, b, in_sem.at[i]) for i, (a, b) in enumerate(zip(sources, places))]
    for load in loads:
        load.start()

    barrier = pltpu.get_barrier_semaphore()
    for k in range(1, members):
        pl.semaphore_signal(barrier, inc=1, device_id={"ens": lax.rem(me + k, members)},
                            device_id_type=pl.DeviceIdType.MESH)
    for k in range(1, bands):
        pl.semaphore_signal(barrier, inc=1, device_id={"band": lax.rem(band + k, bands)},
                            device_id_type=pl.DeviceIdType.MESH)

    def edge_rows(n_side, rows):
        q = iota((2 * n_side, ch * rows), 0)
        lower = q >= n_side
        t = jnp.where(lower, q - n_side, q)
        depth = jnp.where(t >= ch, 1, 0)
        row = jnp.where(lower, rows - 1 - depth, depth)
        return onehot(iota((2 * n_side, ch * rows), 1) == (t & (ch - 1)) * rows + row)

    sel_state, sel_noise, sel_coarse = edge_rows(2 * ch, hf), edge_rows(ch, hf), edge_rows(2 * ch, hc)
    n_base = n_p * 2 * ch
    c_base = n_base + n_p * ch
    picked_noise = []
    for load in loads[:3]:
        load.wait()
    for p in range(n_p):
        rows = mm(sel_state, fine[p]).astype(BF16)
        halo_tx[0, pl.ds(p * 2 * ch, 2 * ch), :] = rows[: 2 * ch]
        halo_tx[1, pl.ds(p * 2 * ch, 2 * ch), :] = rows[2 * ch :]
        picked_noise.append(mm(sel_noise, noise[0, p]))
    for side in range(2):
        halo_tx[side, pl.ds(n_base, n_p * ch), :] = jnp.concatenate(
            [v[side * ch : (side + 1) * ch] for v in picked_noise], axis=0
        ).astype(BF16)
    c0 = jnp.concatenate([coarse[pl.ds(p * rc, rc), :] for p in range(n_p)], axis=1)
    rows = mm(sel_coarse, c0).astype(BF16)
    halo_tx[0, pl.ds(c_base, 2 * ch), :] = rows[: 2 * ch]
    halo_tx[1, pl.ds(c_base, 2 * ch), :] = rows[2 * ch :]

    pl.semaphore_wait(barrier, members + bands - 2)

    up, down = lax.max(band - 1, 0), lax.min(band + 1, bands - 1)
    has_up, has_down = band > 0, band < bands - 1

    def pair(tx, rx, send, recv, side):
        return copy_to(tx.at[side], rx.at[1 - side], send.at[side], recv.at[1 - side],
                       {"band": up if side == 0 else down})

    halo = [pair(halo_tx, halo_rx, h_send, h_recv, side) for side in range(2)]
    edge = [pair(edge_tx, edge_rx, e_send, e_recv, side) for side in range(2)]

    @pl.when(has_up)
    def _():
        halo[0].start()

    @pl.when(has_down)
    def _():
        halo[1].start()

    r4 = hf // hc
    q = iota((rc + 2 * ch, rf), 0)
    cell_c = jnp.where(q < rc, q >> int(math.log2(hc)), (q - rc) & (ch - 1))
    cell_r = jnp.where(q < rc, q & (hc - 1), jnp.where(q < rc + ch, 0, hc - 1))
    src = iota((rc + 2 * ch, rf), 1)
    gather_rows = onehot((src >> int(math.log2(r4))) == cell_c * hc + cell_r)
    l4 = lon // lonc
    fold = onehot((iota((lon, lonc), 0) >> int(math.log2(l4))) == iota((lon, lonc), 1))
    sums = jnp.concatenate(
        [mm(gather_rows, noise[s, p]) for s in range(2) for p in range(n_p)], axis=0
    )
    hi = sums.astype(BF16)
    rest = sums - hi.astype(F32)
    mid = rest.astype(BF16)
    low = (rest - mid.astype(F32)).astype(BF16)
    scale_r = 4.0 / (r4 * l4)
    folded = (mm(hi, fold) + (mm(mid, fold) + mm(low, fold))) * scale_r
    block = rc + 2 * ch

    def forcing_rows(step, lo, n):
        return jnp.concatenate(
            [folded[(step * n_p + p) * block + lo : (step * n_p + p) * block + lo + n] for p in range(n_p)],
            axis=1,
        )

    edge_tx[0] = forcing_rows(0, rc, ch)
    edge_tx[1] = forcing_rows(0, rc + ch, ch)

    @pl.when(has_up)
    def _():
        edge[0].start()

    @pl.when(has_down)
    def _():
        edge[1].start()

    for load in loads[3:]:
        load.wait()
    lane_w = par_v.shape[1]
    lanes = iota((total, total), 1)
    subs = iota((total, total), 0)
    ends = jnp.sum(jnp.where(lanes <= subs, offs[...], 0), axis=1, keepdims=True)
    parent = jnp.sum(jnp.where(ends <= lanes, 1, 0), axis=0, keepdims=True)
    slot_col = jnp.sum(jnp.where(dest[...] == subs, parent, 0), axis=1, keepdims=True)
    par_v[...] = jnp.sum(
        jnp.where(iota((total, lane_w), 0) == iota((total, lane_w), 1), jnp.minimum(slot_col, total - 1), 0),
        axis=0, keepdims=True,
    )
    to_smem = pltpu.make_async_copy(par_v, par_s, loc.at[0])
    to_smem.start()

    w1 = conv_matrix(kf[...], ch, hf, 1, 2)
    w2 = conv_matrix(kf[...], ch, hf, 0, 1)
    w1c = conv_matrix(kc[...], ch, hc, 1, 2)
    w2c = conv_matrix(kc[...], ch, hc, 0, 1)
    pf = jnp.sum(jnp.where(iota((rf, hf), 1) == (iota((rf, hf), 0) & (hf - 1)), prec_f[...], 0.0), axis=1, keepdims=True)
    pc = jnp.sum(jnp.where(iota((rc, hc), 1) == (iota((rc, hc), 0) & (hc - 1)), prec_c[...], 0.0), axis=1, keepdims=True)
    to_smem.wait()

    @pl.when(jnp.logical_not(has_up))
    def _():
        halo_rx[0] = jnp.zeros(halo_rx.shape[1:], BF16)
        edge_rx[0] = jnp.zeros(edge_rx.shape[1:], F32)

    @pl.when(jnp.logical_not(has_down))
    def _():
        halo_rx[1] = jnp.zeros(halo_rx.shape[1:], BF16)
        edge_rx[1] = jnp.zeros(edge_rx.shape[1:], F32)

    def pair_wait(pairs, which):
        for side in range(2):
            @pl.when((has_up, has_down)[side])
            def _():
                if which == "recv":
                    pairs[1 - side].wait_recv()
                else:
                    pairs[side].wait_send()

    pair_wait(halo, "recv")

    q = iota((ch * (hf + 2), 1), 0)
    keep_f = jnp.logical_and(
        jnp.logical_or(has_up, jnp.logical_or(q < rf, q >= rf + ch)), jnp.logical_or(has_down, q < rf + ch)
    )
    q = iota((ch * (hc + 2), 1), 0)
    keep_c = jnp.logical_and(
        jnp.logical_or(has_up, jnp.logical_or(q < rc, q >= rc + ch)), jnp.logical_or(has_down, q < rc + ch)
    )

    def two_steps(own, above, below, force0, force1, wa, wb, keep, width):
        x = jnp.concatenate([own, above, below], axis=0)
        mixed = mm(wa, shifted(x, width))
        base = jnp.concatenate([own, above[:ch], below[:ch]], axis=0)
        y = (base + 0.5 * jnp.tanh(mixed + force0)).astype(BF16).astype(F32)
        y = jnp.where(keep, y, 0.0)
        mixed = mm(wb, shifted(y, width))
        return (y[: own.shape[0]] + 0.5 * jnp.tanh(mixed + force1)).astype(BF16)

    lane = iota((1, TILE_L), 1)
    like = jnp.zeros((1, TILE_L), F32)
    scale_f = -0.5 / math.sqrt(ch * hf * bands * lon)
    scale_c = -0.5 / math.sqrt(ch * hc * bands * lonc)

    send1, own1 = [], []
    batch = n_p // 2
    part1 = lambda ref, first, b: ref.at[pl.ds(first * n_p + b * batch, batch)]

    def share1(share, b):
        row = pl.multiple_of((share // lane_blocks) * TILE_R, TILE_R)
        at = pl.multiple_of((share % lane_blocks) * TILE_L, TILE_L)
        return fin.at[pl.ds(b * batch, batch), pl.ds(row, TILE_R), pl.ds(at, TILE_L)]

    for p in range(n_p):
        hs = [halo_rx[side, pl.ds(p * 2 * ch, 2 * ch), :].astype(F32) for side in range(2)]
        ns = [halo_rx[side, pl.ds(n_base + (p // 2) * 2 * ch, 2 * ch), :].astype(F32)[(p % 2) * ch : (p % 2 + 1) * ch]
              for side in range(2)]
        force0 = jnp.concatenate([noise[0, p].astype(F32), ns[0], ns[1]], axis=0)
        new = two_steps(fine[p].astype(F32), hs[0], hs[1], force0, noise[1, p].astype(F32), w1, w2, keep_f, lon)
        fin[p] = new
        diff = new.astype(F32) - obs_f[...].astype(F32)
        rows = jnp.sum(diff * diff, axis=1, keepdims=True)
        like = like + jnp.where(lane == p, scale_f * jnp.sum(rows * pf, axis=0, keepdims=True), 0.0)

        if (p + 1) % batch == 0:
            b = p // batch
            for k in range(1, members):
                peer = lax.rem(me + k, members)
                send1.append(copy_to(share1(lax.rem(peer, shares), b), part1(recv1, me, b),
                                     s1.at[b * members + k], r1.at[b * members + k], {"ens": peer}))
                send1[-1].start()
            own1.append(pltpu.make_async_copy(share1(rank, b), part1(recv1, me, b), loc.at[2 + b]))
            own1[-1].start()

    pair_wait(edge, "recv")
    hs = [halo_rx[side, pl.ds(c_base, 2 * ch), :].astype(F32) for side in range(2)]
    force0 = jnp.concatenate([forcing_rows(0, 0, rc), edge_rx[0], edge_rx[1]], axis=0)
    new = two_steps(c0.astype(F32), hs[0], hs[1], force0, forcing_rows(1, 0, rc), w1c, w2c, keep_c, lonc)
    parts = []
    for p in range(n_p):
        mine = new[:, p * lonc : (p + 1) * lonc]
        parts.append(mine)
        diff = mine.astype(F32) - obs_c[...].astype(F32)
        rows = jnp.sum(diff * diff, axis=1, keepdims=True)
        like = like + jnp.where(lane == n_p + p, scale_c * jnp.sum(rows * pc, axis=0, keepdims=True), 0.0)
    likeb[band] = jnp.broadcast_to(like, likeb.shape[1:])
    send_b = []
    for k in range(1, bands):
        peer = lax.rem(band + k, bands)
        send_b.append(copy_to(likeb.at[band], likeb.at[band], bs.at[k], br.at[k], {"band": peer}))
        send_b[-1].start()

    n = n_p * rc
    lp = int(math.log2(piece))
    q = iota((n, n), 0)
    src = ((q >> lp) & (n_p - 1)) * rc + (q >> int(math.log2(n_p * piece))) * piece + (q & (piece - 1))
    cstage[...] = mm(onehot(iota((n, n), 1) == src), jnp.concatenate(parts, axis=0)).astype(BF16).reshape(cstage.shape)
    send_c = []
    for g in range(members // shares):
        for c in range(holders):
            peer = g * shares + holder(c)
            send_c.append((peer, copy_to(cstage.at[c], recvc.at[pl.ds(me * TILE_R, TILE_R)],
                                         cs1.at[g * holders + c], cr1.at[lax.rem(peer - me + members, members)],
                                         {"ens": peer})))
    for peer, desc in send_c:
        @pl.when(me != peer)
        def _():
            desc.start()

    for c in range(holders):
        @pl.when(rank == holder(c))
        def _():
            own = pltpu.make_async_copy(cstage.at[c], recvc.at[pl.ds(me * TILE_R, TILE_R)], loc.at[1])
            own.start()
            own.wait()

    for b in range(2):
        own1[b].wait()
        for k in range(1, members):
            copy_to(share1(rank, b), part1(recv1, lax.rem(me - k + members, members), b),
                    s1.at[b * members + k], r1.at[b * members + k],
                    {"ens": lax.rem(me + k, members)}).wait_recv()
    send2 = []
    for k in list(range(1, shares)) + [0]:
        target = lax.rem(rank + k, shares)
        for s in range(n_p):
            slot = target * n_p + s
            chosen[slot] = recv1[par_s[0, group * n_p + slot]]
        from_ref = chosen.at[pl.ds(target * n_p, n_p)]
        if k:
            send2.append(copy_to(from_ref, tile(out_f, rank), s2.at[k], r2.at[k], {"ens": group + target}))
            send2[-1].start()
        else:
            own2 = pltpu.make_async_copy(from_ref, tile(out_f, rank), loc.at[0])
            own2.start()

    for k in range(1, bands):
        src_band = lax.rem(band - k + bands, bands)
        copy_to(likeb.at[src_band], likeb.at[src_band], bs.at[k], br.at[k],
                {"band": lax.rem(band + k, bands)}).wait_recv()
    whole = likeb[0]
    for b in range(1, bands):
        whole = whole + likeb[b]
    whole = whole[:1]
    likee[me] = whole
    send_l = []
    for k in range(1, members):
        send_l.append(copy_to(likee.at[me], likee.at[me], ls.at[k], lr.at[k], {"ens": lax.rem(me + k, members)}))
        send_l[-1].start()

    is_holder = functools.reduce(jnp.logical_or, [rank == holder(c) for c in range(holders)])
    n_slots = shares * n_p

    @pl.when(is_holder)
    def _():
        for k in range(1, members):
            copy_to(cstage.at[0], recvc.at[pl.ds(lax.rem(me - k + members, members) * TILE_R, TILE_R)],
                    cs1.at[0], cr1.at[k], {"ens": lax.rem(me + k, members)}).wait_recv()
        want = group * n_p + (iota((n_slots * piece, total), 0) >> lp)
        who = jnp.sum(jnp.where(dest[...] == want, parent, 0), axis=1, keepdims=True)
        inner = iota((n_slots * piece, 1), 0) & (piece - 1)
        pick = onehot(iota((n_slots * piece, total * piece), 1) == who * piece + inner)
        cchosen[...] = mm(pick, recvc[...]).astype(BF16).reshape(cchosen.shape)

    for c in range(holders):
        @pl.when(rank == holder(c))
        def _():
            for k in range(1, shares):
                target = lax.rem(rank + k, shares)
                copy_to(cchosen.at[target], recvc2.at[pl.ds(c * TILE_R, TILE_R)], cs2.at[k], cr2.at[c],
                        {"ens": group + target}).start()
            own = pltpu.make_async_copy(cchosen.at[rank], recvc2.at[pl.ds(c * TILE_R, TILE_R)], loc.at[1])
            own.start()
            own.wait()

    for k in range(1, members):
        src_m = lax.rem(me - k + members, members)
        copy_to(likee.at[src_m], likee.at[src_m], ls.at[k], lr.at[k], {"ens": lax.rem(me + k, members)}).wait_recv()
    everyone = likee[...].reshape(members, TILE_L)
    lane_all = iota((members, TILE_L), 1)
    for first, out in ((0, out_lf), (n_p, out_lc)):
        here = jnp.logical_and(lane_all >= first, lane_all < first + n_p)
        vals = jnp.where(here, everyone, -jnp.inf)
        peak = jnp.max(jnp.max(vals, axis=1, keepdims=True), axis=0, keepdims=True)
        part = jnp.where(here, jnp.exp(vals - peak), 0.0)
        norm = jnp.sum(jnp.sum(part, axis=1, keepdims=True), axis=0, keepdims=True)
        out[...] = (whole - (peak + jnp.log(norm)))[:, first : first + n_p]

    for c in range(holders):
        @pl.when(rank != holder(c))
        def _():
            copy_to(cchosen.at[0], recvc2.at[pl.ds(c * TILE_R, TILE_R)], cs2.at[0], cr2.at[c],
                    {"ens": group + holder(c)}).wait_recv()
    q = iota((n, n), 0)
    row = q & (rc - 1)
    src = (row >> lp) * (n_p * piece) + (q >> int(math.log2(rc))) * piece + (row & (piece - 1))
    out_c[...] = mm(onehot(iota((n, n), 1) == src), recvc2[...]).astype(BF16)

    own2.wait()
    for k in range(1, shares):
        source = lax.rem(rank - k + shares, shares)
        copy_to(chosen.at[pl.ds(0, n_p)], tile(out_f, source), s2.at[k], r2.at[k],
                {"ens": group + lax.rem(rank + k, shares)}).wait_recv()

    pair_wait(halo, "send")
    pair_wait(edge, "send")
    for desc in send1 + send2 + send_b + send_l:
        desc.wait_send()
    for peer, desc in send_c:
        @pl.when(me != peer)
        def _():
            desc.wait_send()

    @pl.when(is_holder)
    def _():
        for k in range(1, shares):
            copy_to(cchosen.at[0], recvc2.at[pl.ds(0, TILE_R)], cs2.at[k], cr2.at[0],
                    {"ens": group + lax.rem(rank + k, shares)}).wait_send()


def write_out(*refs):
    count = (len(refs) - 1) // 2
    copies = [pltpu.make_async_copy(refs[i], refs[count + i], refs[-1].at[i]) for i in range(count)]
    for copy in copies:
        copy.start()
    for copy in copies:
        copy.wait()


def shards(fine, coarse, noise, kf, kc, obs_f, obs_c, prec_f, prec_c, offspring, dest_slot):
    bands, members = lax.axis_size("band"), lax.axis_size("ens")
    n_p, ch, hf, lon = fine.shape
    hc, lonc = coarse.shape[2:]
    rf, rc = ch * hf, ch * hc
    total = offspring.shape[0]
    shares = (rf // TILE_R) * (lon // TILE_L)
    holders = n_p * rc // TILE_R
    groups = members // shares
    lane_w = -(-total // TILE_L) * TILE_L
    halo_rows = n_p * 3 * ch + 2 * ch
    dma = pltpu.SemaphoreType.DMA
    vmem = pl.BlockSpec(memory_space=pltpu.VMEM)
    hbm = pl.BlockSpec(memory_space=pl.ANY)
    args = (
        fine.reshape(n_p, rf, lon),
        coarse.reshape(n_p * rc, lonc),
        noise.reshape(2, n_p, rf, lon),
        kf, kc,
        obs_f.reshape(rf, lon),
        obs_c.reshape(rc, lonc),
        prec_f.reshape(1, hf),
        prec_c.reshape(1, hc),
        offspring.reshape(1, total),
        dest_slot.reshape(1, total),
    )
    results = (
        jax.ShapeDtypeStruct((n_p, rf, lon), BF16),
        jax.ShapeDtypeStruct((n_p * rc, lonc), BF16),
        jax.ShapeDtypeStruct((1, n_p), F32),
        jax.ShapeDtypeStruct((1, n_p), F32),
    )
    done = pl.pallas_call(
        functools.partial(kernel, bands, members),
        out_shape=tuple(pltpu.VMEM(r.shape, r.dtype) for r in results),
        in_specs=[hbm] * 11,
        out_specs=(vmem,) * 4,
        scratch_shapes=[pltpu.VMEM(a.shape, a.dtype) for a in args] + [
            dma((11,)),
            pltpu.VMEM((2, halo_rows, lon), BF16),
            pltpu.VMEM((2, halo_rows, lon), BF16),
            pltpu.VMEM((2, ch, n_p * lonc), F32),
            pltpu.VMEM((2, ch, n_p * lonc), F32),
            pltpu.VMEM((n_p, rf, lon), BF16),
            pltpu.VMEM((total, TILE_R, TILE_L), BF16),
            pltpu.VMEM((shares * n_p, TILE_R, TILE_L), BF16),
            pltpu.VMEM((holders, TILE_R, TILE_L), BF16),
            pltpu.VMEM((members * TILE_R, TILE_L), BF16),
            pltpu.VMEM((shares, TILE_R, TILE_L), BF16),
            pltpu.VMEM((holders * TILE_R, TILE_L), BF16),
            pltpu.VMEM((bands, 8, TILE_L), F32),
            pltpu.VMEM((members, 1, TILE_L), F32),
            pltpu.VMEM((1, lane_w), I32),
            pltpu.SMEM((1, lane_w), I32),
            dma((2,)), dma((2,)), dma((2,)), dma((2,)),
            dma((2 * members,)), dma((2 * members,)), dma((shares,)), dma((shares,)),
            dma((groups * holders,)), dma((members,)), dma((shares,)), dma((holders,)),
            dma((bands,)), dma((bands,)), dma((members,)), dma((members,)), dma((4,)),
        ],
        compiler_params=pltpu.CompilerParams(
            collective_id=0, has_side_effects=True, vmem_limit_bytes=VMEM_LIMIT
        ),
    )(*args)
    of, oc, lf, lc = pl.pallas_call(
        write_out,
        out_shape=results,
        in_specs=[vmem] * 4,
        out_specs=(hbm,) * 4,
        scratch_shapes=[dma((4,))],
        compiler_params=pltpu.CompilerParams(vmem_limit_bytes=4 * 1024 * 1024),
    )(*[pltpu.with_memory_space_constraint(d, pltpu.VMEM) for d in done])
    return (
        of.reshape(n_p, ch, hf, lon),
        oc.reshape(n_p, ch, hc, lonc),
        lf.reshape(n_p),
        lc.reshape(n_p),
    )


def solution(mesh):
    return jax.shard_map(
        shards,
        mesh=mesh,
        in_specs=(
            P("ens", None, "band", None),
            P("ens", None, "band", None),
            P(None, "ens", None, "band", None),
            P(),
            P(),
            P(None, "band", None),
            P(None, "band", None),
            P("band"),
            P("band"),
            P(),
            P(),
        ),
        out_specs=(P("ens", None, "band", None), P("ens", None, "band", None), P("ens"), P("ens")),
        check_vma=False,
    )
```

```python
import functools
import math

import jax
import jax.numpy as jnp
from jax import lax
from jax.experimental import pallas as pl
from jax.experimental.pallas import tpu as pltpu
from jax.sharding import PartitionSpec as P

F32 = jnp.float32
BF16 = jnp.bfloat16
I32 = jnp.int32
TILE_R = 16
TILE_L = 128
VMEM_LIMIT = 56 * 1024 * 1024


def iota(shape, dim):
    return lax.broadcasted_iota(I32, shape, dim)


def onehot(cond):
    return jnp.where(cond, 1.0, 0.0).astype(BF16)


def mm(a, b):
    return jnp.dot(a, b, preferred_element_type=F32)


def layout(idx, ch, rows, halo):
    base = ch * rows
    own_c, own_r = idx >> int(math.log2(rows)), idx & (rows - 1)
    if halo == 0:
        return own_c, own_r
    up = idx - base
    down = up - halo * ch
    above = -1 - jnp.where(up >= ch, 1, 0)
    below = rows + jnp.where(down >= ch, 1, 0)
    side_c = up & (ch - 1)
    side_r = jnp.where(down < 0, above, below)
    return jnp.where(idx < base, own_c, side_c), jnp.where(idx < base, own_r, side_r)


def conv_matrix(kern, ch, rows, halo_out, halo_in):
    n_out = ch * (rows + 2 * halo_out)
    n_in = ch * (rows + 2 * halo_in)
    o, r_out = layout(iota((n_out, 1), 0), ch, rows, halo_out)
    col = iota((1, 3 * n_in), 1)
    shift = jnp.where(col >= n_in, 1, 0) + jnp.where(col >= 2 * n_in, 1, 0)
    i, r_in = layout(col - n_in * shift, ch, rows, halo_in)
    spread = mm(onehot(o == iota((n_out, ch), 1)), kern).astype(BF16)
    taps = iota((9 * ch, 3 * n_in), 0)
    total = None
    for a in range(3):
        pick = mm(spread, onehot(taps == 9 * i + 3 * a + shift))
        term = jnp.where(r_in - r_out + 1 == a, pick, 0.0)
        total = term if total is None else total + term
    return total.astype(BF16)


def shifted(x, width):
    parts = [x[:, j : j + width] for j in range(0, x.shape[1], width)]
    left = [pltpu.roll(v, 1, 1) for v in parts]
    right = [pltpu.roll(v, width - 1, 1) for v in parts]
    join = lambda vs: vs[0] if len(vs) == 1 else jnp.concatenate(vs, axis=1)
    return jnp.concatenate([join(left), x, join(right)], axis=0).astype(BF16)


def far_first(count):
    return sorted(range(1, count), key=lambda k: (abs(k - count // 2), k))


def kernel(
    bands, members,
    fine_h, coarse_h, noise_h, kf_h, kc_h, obs_f_h, obs_c_h, prec_f_h, prec_c_h, offs_h, dest_h,
    out_f, out_c, out_lf, out_lc,
    fine, coarse, noise, kf, kc, obs_f, obs_c, prec_f, prec_c, offs, dest, in_sem,
    halo_tx, halo_rx, edge_tx, edge_rx, fin, recv1, chosen, cstage, recvc, cchosen, recvc2,
    likeb, likee, par_v, par_s,
    h_send, h_recv, e_send, e_recv, s1, r1, s2, r2, cs1, cr1, cs2, cr2, bs, br, ls, lr, loc,
):
    band = lax.axis_index("band")
    me = lax.axis_index("ens")
    n_p, ch, hf, lon = fine.shape[0], kf.shape[0], prec_f.shape[1], fine.shape[2]
    hc, lonc = prec_c.shape[1], coarse.shape[1]
    rf, rc = ch * hf, ch * hc
    lane_blocks = lon // TILE_L
    shares = (rf // TILE_R) * lane_blocks
    holders = n_p * rc // TILE_R
    piece = rc // holders
    total = offs.shape[1]
    group = (me // shares) * shares
    rank = me - group

    def holder(c):
        return c * (shares // holders) + (c % 2) * (shares // holders // 2)

    def tile(ref, share):
        row = pl.multiple_of((share // lane_blocks) * TILE_R, TILE_R)
        lane = pl.multiple_of((share % lane_blocks) * TILE_L, TILE_L)
        return ref.at[:, pl.ds(row, TILE_R), pl.ds(lane, TILE_L)]

    def copy_to(src, dst, send, recv, device):
        return pltpu.make_async_remote_copy(
            src_ref=src, dst_ref=dst, send_sem=send, recv_sem=recv,
            device_id=device, device_id_type=pl.DeviceIdType.MESH,
        )

    sources = (fine_h, noise_h, coarse_h, kf_h, kc_h, obs_f_h, obs_c_h, prec_f_h, prec_c_h, offs_h, dest_h)
    places = (fine, noise, coarse, kf, kc, obs_f, obs_c, prec_f, prec_c, offs, dest)
    loads = [pltpu.make_async_copy(a, b, in_sem.at[i]) for i, (a, b) in enumerate(zip(sources, places))]
    for load in loads:
        load.start()

    barrier = pltpu.get_barrier_semaphore()
    for k in range(1, members):
        pl.semaphore_signal(barrier, inc=1, device_id={"ens": lax.rem(me + k, members)},
                            device_id_type=pl.DeviceIdType.MESH)
    for k in range(1, bands):
        pl.semaphore_signal(barrier, inc=1, device_id={"band": lax.rem(band + k, bands)},
                            device_id_type=pl.DeviceIdType.MESH)

    def edge_rows(n_side, rows):
        q = iota((2 * n_side, ch * rows), 0)
        lower = q >= n_side
        t = jnp.where(lower, q - n_side, q)
        depth = jnp.where(t >= ch, 1, 0)
        row = jnp.where(lower, rows - 1 - depth, depth)
        return onehot(iota((2 * n_side, ch * rows), 1) == (t & (ch - 1)) * rows + row)

    sel_state, sel_noise, sel_coarse = edge_rows(2 * ch, hf), edge_rows(ch, hf), edge_rows(2 * ch, hc)
    n_base = n_p * 2 * ch
    c_base = n_base + n_p * ch
    picked_noise = []
    for load in loads[:3]:
        load.wait()
    for p in range(n_p):
        rows = mm(sel_state, fine[p]).astype(BF16)
        halo_tx[0, pl.ds(p * 2 * ch, 2 * ch), :] = rows[: 2 * ch]
        halo_tx[1, pl.ds(p * 2 * ch, 2 * ch), :] = rows[2 * ch :]
        picked_noise.append(mm(sel_noise, noise[0, p]))
    for side in range(2):
        halo_tx[side, pl.ds(n_base, n_p * ch), :] = jnp.concatenate(
            [v[side * ch : (side + 1) * ch] for v in picked_noise], axis=0
        ).astype(BF16)
    c0 = jnp.concatenate([coarse[pl.ds(p * rc, rc), :] for p in range(n_p)], axis=1)
    rows = mm(sel_coarse, c0).astype(BF16)
    halo_tx[0, pl.ds(c_base, 2 * ch), :] = rows[: 2 * ch]
    halo_tx[1, pl.ds(c_base, 2 * ch), :] = rows[2 * ch :]

    pl.semaphore_wait(barrier, members + bands - 2)

    up, down = lax.max(band - 1, 0), lax.min(band + 1, bands - 1)
    has_up, has_down = band > 0, band < bands - 1

    def pair(tx, rx, send, recv, side):
        return copy_to(tx.at[side], rx.at[1 - side], send.at[side], recv.at[1 - side],
                       {"band": up if side == 0 else down})

    halo = [pair(halo_tx, halo_rx, h_send, h_recv, side) for side in range(2)]
    edge = [pair(edge_tx, edge_rx, e_send, e_recv, side) for side in range(2)]

    @pl.when(has_up)
    def _():
        halo[0].start()

    @pl.when(has_down)
    def _():
        halo[1].start()

    r4 = hf // hc
    q = iota((rc + 2 * ch, rf), 0)
    cell_c = jnp.where(q < rc, q >> int(math.log2(hc)), (q - rc) & (ch - 1))
    cell_r = jnp.where(q < rc, q & (hc - 1), jnp.where(q < rc + ch, 0, hc - 1))
    src = iota((rc + 2 * ch, rf), 1)
    gather_rows = onehot((src >> int(math.log2(r4))) == cell_c * hc + cell_r)
    l4 = lon // lonc
    fold = onehot((iota((lon, lonc), 0) >> int(math.log2(l4))) == iota((lon, lonc), 1))
    sums = jnp.concatenate(
        [mm(gather_rows, noise[s, p]) for s in range(2) for p in range(n_p)], axis=0
    )
    hi = sums.astype(BF16)
    rest = sums - hi.astype(F32)
    mid = rest.astype(BF16)
    low = (rest - mid.astype(F32)).astype(BF16)
    scale_r = 4.0 / (r4 * l4)
    folded = (mm(hi, fold) + (mm(mid, fold) + mm(low, fold))) * scale_r
    block = rc + 2 * ch

    def forcing_rows(step, lo, n):
        return jnp.concatenate(
            [folded[(step * n_p + p) * block + lo : (step * n_p + p) * block + lo + n] for p in range(n_p)],
            axis=1,
        )

    edge_tx[0] = forcing_rows(0, rc, ch)
    edge_tx[1] = forcing_rows(0, rc + ch, ch)

    @pl.when(has_up)
    def _():
        edge[0].start()

    @pl.when(has_down)
    def _():
        edge[1].start()

    for load in loads[3:]:
        load.wait()
    lane_w = par_v.shape[1]
    lanes = iota((total, total), 1)
    subs = iota((total, total), 0)
    ends = jnp.sum(jnp.where(lanes <= subs, offs[...], 0), axis=1, keepdims=True)
    parent = jnp.sum(jnp.where(ends <= lanes, 1, 0), axis=0, keepdims=True)
    slot_col = jnp.sum(jnp.where(dest[...] == subs, parent, 0), axis=1, keepdims=True)
    par_v[...] = jnp.sum(
        jnp.where(iota((total, lane_w), 0) == iota((total, lane_w), 1), jnp.minimum(slot_col, total - 1), 0),
        axis=0, keepdims=True,
    )
    to_smem = pltpu.make_async_copy(par_v, par_s, loc.at[0])
    to_smem.start()

    w1 = conv_matrix(kf[...], ch, hf, 1, 2)
    w2 = conv_matrix(kf[...], ch, hf, 0, 1)
    w1c = conv_matrix(kc[...], ch, hc, 1, 2)
    w2c = conv_matrix(kc[...], ch, hc, 0, 1)
    pf = jnp.sum(jnp.where(iota((rf, hf), 1) == (iota((rf, hf), 0) & (hf - 1)), prec_f[...], 0.0), axis=1, keepdims=True)
    pc = jnp.sum(jnp.where(iota((rc, hc), 1) == (iota((rc, hc), 0) & (hc - 1)), prec_c[...], 0.0), axis=1, keepdims=True)
    to_smem.wait()

    @pl.when(jnp.logical_not(has_up))
    def _():
        halo_rx[0] = jnp.zeros(halo_rx.shape[1:], BF16)
        edge_rx[0] = jnp.zeros(edge_rx.shape[1:], F32)

    @pl.when(jnp.logical_not(has_down))
    def _():
        halo_rx[1] = jnp.zeros(halo_rx.shape[1:], BF16)
        edge_rx[1] = jnp.zeros(edge_rx.shape[1:], F32)

    def pair_wait(pairs, which):
        for side in range(2):
            @pl.when((has_up, has_down)[side])
            def _():
                if which == "recv":
                    pairs[1 - side].wait_recv()
                else:
                    pairs[side].wait_send()

    pair_wait(halo, "recv")

    q = iota((ch * (hf + 2), 1), 0)
    keep_f = jnp.logical_and(
        jnp.logical_or(has_up, jnp.logical_or(q < rf, q >= rf + ch)), jnp.logical_or(has_down, q < rf + ch)
    )
    q = iota((ch * (hc + 2), 1), 0)
    keep_c = jnp.logical_and(
        jnp.logical_or(has_up, jnp.logical_or(q < rc, q >= rc + ch)), jnp.logical_or(has_down, q < rc + ch)
    )

    def two_steps(own, above, below, force0, force1, wa, wb, keep, width):
        x = jnp.concatenate([own, above, below], axis=0)
        mixed = mm(wa, shifted(x, width))
        base = jnp.concatenate([own, above[:ch], below[:ch]], axis=0)
        y = (base + 0.5 * jnp.tanh(mixed + force0)).astype(BF16).astype(F32)
        y = jnp.where(keep, y, 0.0)
        mixed = mm(wb, shifted(y, width))
        return (y[: own.shape[0]] + 0.5 * jnp.tanh(mixed + force1)).astype(BF16)

    lane = iota((1, TILE_L), 1)
    like = jnp.zeros((1, TILE_L), F32)
    scale_f = -0.5 / math.sqrt(ch * hf * bands * lon)
    scale_c = -0.5 / math.sqrt(ch * hc * bands * lonc)

    send1, own1 = [], []
    batch = n_p // 2
    part1 = lambda ref, first, b: ref.at[pl.ds(first * n_p + b * batch, batch)]

    def share1(share, b):
        row = pl.multiple_of((share // lane_blocks) * TILE_R, TILE_R)
        at = pl.multiple_of((share % lane_blocks) * TILE_L, TILE_L)
        return fin.at[pl.ds(b * batch, batch), pl.ds(row, TILE_R), pl.ds(at, TILE_L)]

    for p in range(n_p):
        hs = [halo_rx[side, pl.ds(p * 2 * ch, 2 * ch), :].astype(F32) for side in range(2)]
        ns = [halo_rx[side, pl.ds(n_base + (p // 2) * 2 * ch, 2 * ch), :].astype(F32)[(p % 2) * ch : (p % 2 + 1) * ch]
              for side in range(2)]
        force0 = jnp.concatenate([noise[0, p].astype(F32), ns[0], ns[1]], axis=0)
        new = two_steps(fine[p].astype(F32), hs[0], hs[1], force0, noise[1, p].astype(F32), w1, w2, keep_f, lon)
        fin[p] = new
        diff = new.astype(F32) - obs_f[...].astype(F32)
        rows = jnp.sum(diff * diff, axis=1, keepdims=True)
        like = like + jnp.where(lane == p, scale_f * jnp.sum(rows * pf, axis=0, keepdims=True), 0.0)

        if (p + 1) % batch == 0:
            b = p // batch
            for k in far_first(members):
                peer = lax.rem(me + k, members)
                send1.append(copy_to(share1(lax.rem(peer, shares), b), part1(recv1, me, b),
                                     s1.at[b * members + k], r1.at[b * members + k], {"ens": peer}))
                send1[-1].start()
            own1.append(pltpu.make_async_copy(share1(rank, b), part1(recv1, me, b), loc.at[2 + b]))
            own1[-1].start()

    pair_wait(edge, "recv")
    hs = [halo_rx[side, pl.ds(c_base, 2 * ch), :].astype(F32) for side in range(2)]
    force0 = jnp.concatenate([forcing_rows(0, 0, rc), edge_rx[0], edge_rx[1]], axis=0)
    new = two_steps(c0.astype(F32), hs[0], hs[1], force0, forcing_rows(1, 0, rc), w1c, w2c, keep_c, lonc)
    parts = []
    for p in range(n_p):
        mine = new[:, p * lonc : (p + 1) * lonc]
        parts.append(mine)
        diff = mine.astype(F32) - obs_c[...].astype(F32)
        rows = jnp.sum(diff * diff, axis=1, keepdims=True)
        like = like + jnp.where(lane == n_p + p, scale_c * jnp.sum(rows * pc, axis=0, keepdims=True), 0.0)
    likeb[band] = jnp.broadcast_to(like, likeb.shape[1:])
    send_b = []
    for k in range(1, bands):
        peer = lax.rem(band + k, bands)
        send_b.append(copy_to(likeb.at[band], likeb.at[band], bs.at[k], br.at[k], {"band": peer}))
        send_b[-1].start()

    n = n_p * rc
    lp = int(math.log2(piece))
    q = iota((n, n), 0)
    src = ((q >> lp) & (n_p - 1)) * rc + (q >> int(math.log2(n_p * piece))) * piece + (q & (piece - 1))
    cstage[...] = mm(onehot(iota((n, n), 1) == src), jnp.concatenate(parts, axis=0)).astype(BF16).reshape(cstage.shape)
    send_c = []
    for g in range(members // shares):
        for c in range(holders):
            peer = g * shares + holder(c)
            send_c.append((peer, copy_to(cstage.at[c], recvc.at[pl.ds(me * TILE_R, TILE_R)],
                                         cs1.at[g * holders + c], cr1.at[lax.rem(peer - me + members, members)],
                                         {"ens": peer})))
    for peer, desc in send_c:
        @pl.when(me != peer)
        def _():
            desc.start()

    for c in range(holders):
        @pl.when(rank == holder(c))
        def _():
            own = pltpu.make_async_copy(cstage.at[c], recvc.at[pl.ds(me * TILE_R, TILE_R)], loc.at[1])
            own.start()
            own.wait()

    for k in range(1, bands):
        src_band = lax.rem(band - k + bands, bands)
        copy_to(likeb.at[src_band], likeb.at[src_band], bs.at[k], br.at[k],
                {"band": lax.rem(band + k, bands)}).wait_recv()
    whole = likeb[0]
    for b in range(1, bands):
        whole = whole + likeb[b]
    whole = whole[:1]
    likee[me] = whole
    send_l = []
    for k in range(1, members):
        send_l.append(copy_to(likee.at[me], likee.at[me], ls.at[k], lr.at[k], {"ens": lax.rem(me + k, members)}))
        send_l[-1].start()

    for b in range(2):
        own1[b].wait()
        for k in range(1, members):
            copy_to(share1(rank, b), part1(recv1, lax.rem(me - k + members, members), b),
                    s1.at[b * members + k], r1.at[b * members + k],
                    {"ens": lax.rem(me + k, members)}).wait_recv()
    send2 = []
    for k in far_first(shares) + [0]:
        target = lax.rem(rank + k, shares)
        for s in range(n_p):
            slot = target * n_p + s
            chosen[slot] = recv1[par_s[0, group * n_p + slot]]
        from_ref = chosen.at[pl.ds(target * n_p, n_p)]
        if k:
            send2.append(copy_to(from_ref, tile(out_f, rank), s2.at[k], r2.at[k], {"ens": group + target}))
            send2[-1].start()
        else:
            own2 = pltpu.make_async_copy(from_ref, tile(out_f, rank), loc.at[0])
            own2.start()

    is_holder = functools.reduce(jnp.logical_or, [rank == holder(c) for c in range(holders)])
    n_slots = shares * n_p

    @pl.when(is_holder)
    def _():
        want = group * n_p + (iota((n_slots * piece, total), 0) >> lp)
        who = jnp.sum(jnp.where(dest[...] == want, parent, 0), axis=1, keepdims=True)
        inner = iota((n_slots * piece, 1), 0) & (piece - 1)
        pick = onehot(iota((n_slots * piece, total * piece), 1) == who * piece + inner)
        for k in range(1, members):
            copy_to(cstage.at[0], recvc.at[pl.ds(lax.rem(me - k + members, members) * TILE_R, TILE_R)],
                    cs1.at[0], cr1.at[k], {"ens": lax.rem(me + k, members)}).wait_recv()
        cchosen[...] = mm(pick, recvc[...]).astype(BF16).reshape(cchosen.shape)

    for c in range(holders):
        @pl.when(rank == holder(c))
        def _():
            for k in range(1, shares):
                target = lax.rem(rank + k, shares)
                copy_to(cchosen.at[target], recvc2.at[pl.ds(c * TILE_R, TILE_R)], cs2.at[k], cr2.at[c],
                        {"ens": group + target}).start()
            own = pltpu.make_async_copy(cchosen.at[rank], recvc2.at[pl.ds(c * TILE_R, TILE_R)], loc.at[1])
            own.start()
            own.wait()

    for k in range(1, members):
        src_m = lax.rem(me - k + members, members)
        copy_to(likee.at[src_m], likee.at[src_m], ls.at[k], lr.at[k], {"ens": lax.rem(me + k, members)}).wait_recv()
    everyone = likee[...].reshape(members, TILE_L)
    lane_all = iota((members, TILE_L), 1)
    for first, out in ((0, out_lf), (n_p, out_lc)):
        here = jnp.logical_and(lane_all >= first, lane_all < first + n_p)
        vals = jnp.where(here, everyone, -jnp.inf)
        peak = jnp.max(jnp.max(vals, axis=1, keepdims=True), axis=0, keepdims=True)
        part = jnp.where(here, jnp.exp(vals - peak), 0.0)
        norm = jnp.sum(jnp.sum(part, axis=1, keepdims=True), axis=0, keepdims=True)
        out[...] = (whole - (peak + jnp.log(norm)))[:, first : first + n_p]

    for c in range(holders):
        @pl.when(rank != holder(c))
        def _():
            copy_to(cchosen.at[0], recvc2.at[pl.ds(c * TILE_R, TILE_R)], cs2.at[0], cr2.at[c],
                    {"ens": group + holder(c)}).wait_recv()
    q = iota((n, n), 0)
    row = q & (rc - 1)
    src = (row >> lp) * (n_p * piece) + (q >> int(math.log2(rc))) * piece + (row & (piece - 1))
    out_c[...] = mm(onehot(iota((n, n), 1) == src), recvc2[...]).astype(BF16)

    own2.wait()
    for k in range(1, shares):
        source = lax.rem(rank - k + shares, shares)
        copy_to(chosen.at[pl.ds(0, n_p)], tile(out_f, source), s2.at[k], r2.at[k],
                {"ens": group + lax.rem(rank + k, shares)}).wait_recv()

    pair_wait(halo, "send")
    pair_wait(edge, "send")
    for desc in send1 + send2 + send_b + send_l:
        desc.wait_send()
    for peer, desc in send_c:
        @pl.when(me != peer)
        def _():
            desc.wait_send()

    @pl.when(is_holder)
    def _():
        for k in range(1, shares):
            copy_to(cchosen.at[0], recvc2.at[pl.ds(0, TILE_R)], cs2.at[k], cr2.at[0],
                    {"ens": group + lax.rem(rank + k, shares)}).wait_send()


def write_out(*refs):
    count = (len(refs) - 1) // 2
    copies = [pltpu.make_async_copy(refs[i], refs[count + i], refs[-1].at[i]) for i in range(count)]
    for copy in copies:
        copy.start()
    for copy in copies:
        copy.wait()


def shards(fine, coarse, noise, kf, kc, obs_f, obs_c, prec_f, prec_c, offspring, dest_slot):
    bands, members = lax.axis_size("band"), lax.axis_size("ens")
    n_p, ch, hf, lon = fine.shape
    hc, lonc = coarse.shape[2:]
    rf, rc = ch * hf, ch * hc
    total = offspring.shape[0]
    shares = (rf // TILE_R) * (lon // TILE_L)
    holders = n_p * rc // TILE_R
    groups = members // shares
    lane_w = -(-total // TILE_L) * TILE_L
    halo_rows = n_p * 3 * ch + 2 * ch
    dma = pltpu.SemaphoreType.DMA
    vmem = pl.BlockSpec(memory_space=pltpu.VMEM)
    hbm = pl.BlockSpec(memory_space=pl.ANY)
    args = (
        fine.reshape(n_p, rf, lon),
        coarse.reshape(n_p * rc, lonc),
        noise.reshape(2, n_p, rf, lon),
        kf, kc,
        obs_f.reshape(rf, lon),
        obs_c.reshape(rc, lonc),
        prec_f.reshape(1, hf),
        prec_c.reshape(1, hc),
        offspring.reshape(1, total),
        dest_slot.reshape(1, total),
    )
    results = (
        jax.ShapeDtypeStruct((n_p, rf, lon), BF16),
        jax.ShapeDtypeStruct((n_p * rc, lonc), BF16),
        jax.ShapeDtypeStruct((1, n_p), F32),
        jax.ShapeDtypeStruct((1, n_p), F32),
    )
    done = pl.pallas_call(
        functools.partial(kernel, bands, members),
        out_shape=tuple(pltpu.VMEM(r.shape, r.dtype) for r in results),
        in_specs=[hbm] * 11,
        out_specs=(vmem,) * 4,
        scratch_shapes=[pltpu.VMEM(a.shape, a.dtype) for a in args] + [
            dma((11,)),
            pltpu.VMEM((2, halo_rows, lon), BF16),
            pltpu.VMEM((2, halo_rows, lon), BF16),
            pltpu.VMEM((2, ch, n_p * lonc), F32),
            pltpu.VMEM((2, ch, n_p * lonc), F32),
            pltpu.VMEM((n_p, rf, lon), BF16),
            pltpu.VMEM((total, TILE_R, TILE_L), BF16),
            pltpu.VMEM((shares * n_p, TILE_R, TILE_L), BF16),
            pltpu.VMEM((holders, TILE_R, TILE_L), BF16),
            pltpu.VMEM((members * TILE_R, TILE_L), BF16),
            pltpu.VMEM((shares, TILE_R, TILE_L), BF16),
            pltpu.VMEM((holders * TILE_R, TILE_L), BF16),
            pltpu.VMEM((bands, 8, TILE_L), F32),
            pltpu.VMEM((members, 1, TILE_L), F32),
            pltpu.VMEM((1, lane_w), I32),
            pltpu.SMEM((1, lane_w), I32),
            dma((2,)), dma((2,)), dma((2,)), dma((2,)),
            dma((2 * members,)), dma((2 * members,)), dma((shares,)), dma((shares,)),
            dma((groups * holders,)), dma((members,)), dma((shares,)), dma((holders,)),
            dma((bands,)), dma((bands,)), dma((members,)), dma((members,)), dma((4,)),
        ],
        compiler_params=pltpu.CompilerParams(
            collective_id=0, has_side_effects=True, vmem_limit_bytes=VMEM_LIMIT
        ),
    )(*args)
    of, oc, lf, lc = pl.pallas_call(
        write_out,
        out_shape=results,
        in_specs=[vmem] * 4,
        out_specs=(hbm,) * 4,
        scratch_shapes=[dma((4,))],
        compiler_params=pltpu.CompilerParams(vmem_limit_bytes=4 * 1024 * 1024),
    )(*[pltpu.with_memory_space_constraint(d, pltpu.VMEM) for d in done])
    return (
        of.reshape(n_p, ch, hf, lon),
        oc.reshape(n_p, ch, hc, lonc),
        lf.reshape(n_p),
        lc.reshape(n_p),
    )


def solution(mesh):
    return jax.shard_map(
        shards,
        mesh=mesh,
        in_specs=(
            P("ens", None, "band", None),
            P("ens", None, "band", None),
            P(None, "ens", None, "band", None),
            P(),
            P(),
            P(None, "band", None),
            P(None, "band", None),
            P("band"),
            P("band"),
            P(),
            P(),
        ),
        out_specs=(P("ens", None, "band", None), P("ens", None, "band", None), P("ens"), P("ens")),
        check_vma=False,
    )
```

```python
import functools
import math

import jax
import jax.numpy as jnp
from jax import lax
from jax.experimental import pallas as pl
from jax.experimental.pallas import tpu as pltpu
from jax.sharding import PartitionSpec as P

F32 = jnp.float32
BF16 = jnp.bfloat16
I32 = jnp.int32
TILE_R = 16
TILE_L = 128
VMEM_LIMIT = 56 * 1024 * 1024


def iota(shape, dim):
    return lax.broadcasted_iota(I32, shape, dim)


def onehot(cond):
    return jnp.where(cond, 1.0, 0.0).astype(BF16)


def mm(a, b):
    return jnp.dot(a, b, preferred_element_type=F32)


def layout(idx, ch, rows, halo):
    base = ch * rows
    own_c, own_r = idx >> int(math.log2(rows)), idx & (rows - 1)
    if halo == 0:
        return own_c, own_r
    up = idx - base
    down = up - halo * ch
    above = -1 - jnp.where(up >= ch, 1, 0)
    below = rows + jnp.where(down >= ch, 1, 0)
    side_c = up & (ch - 1)
    side_r = jnp.where(down < 0, above, below)
    return jnp.where(idx < base, own_c, side_c), jnp.where(idx < base, own_r, side_r)


def conv_matrix(kern, ch, rows, halo_out, halo_in):
    n_out = ch * (rows + 2 * halo_out)
    n_in = ch * (rows + 2 * halo_in)
    o, r_out = layout(iota((n_out, 1), 0), ch, rows, halo_out)
    col = iota((1, 3 * n_in), 1)
    shift = jnp.where(col >= n_in, 1, 0) + jnp.where(col >= 2 * n_in, 1, 0)
    i, r_in = layout(col - n_in * shift, ch, rows, halo_in)
    spread = mm(onehot(o == iota((n_out, ch), 1)), kern).astype(BF16)
    taps = iota((9 * ch, 3 * n_in), 0)
    total = None
    for a in range(3):
        pick = mm(spread, onehot(taps == 9 * i + 3 * a + shift))
        term = jnp.where(r_in - r_out + 1 == a, pick, 0.0)
        total = term if total is None else total + term
    return total.astype(BF16)


def shifted(x, width):
    parts = [x[:, j : j + width] for j in range(0, x.shape[1], width)]
    left = [pltpu.roll(v, 1, 1) for v in parts]
    right = [pltpu.roll(v, width - 1, 1) for v in parts]
    join = lambda vs: vs[0] if len(vs) == 1 else jnp.concatenate(vs, axis=1)
    return jnp.concatenate([join(left), x, join(right)], axis=0).astype(BF16)


def far_first(count):
    return sorted(range(1, count), key=lambda k: (abs(k - count // 2), k))


def kernel(
    bands, members,
    fine_h, coarse_h, noise_h, kf_h, kc_h, obs_f_h, obs_c_h, prec_f_h, prec_c_h, offs_h, dest_h,
    out_f, out_c, out_lf, out_lc,
    fine, coarse, noise, kf, kc, obs_f, obs_c, prec_f, prec_c, offs, dest, in_sem,
    halo_tx, halo_rx, edge_tx, edge_rx, fin, recv1, chosen, cstage, recvc, cchosen, recvc2,
    likeb, likee, par_v, par_s,
    h_send, h_recv, e_send, e_recv, s1, r1, s2, r2, cs1, cr1, cs2, cr2, bs, br, ls, lr, loc,
):
    band = lax.axis_index("band")
    me = lax.axis_index("ens")
    n_p, ch, hf, lon = fine.shape[0], kf.shape[0], prec_f.shape[1], fine.shape[2]
    hc, lonc = prec_c.shape[1], coarse.shape[1]
    rf, rc = ch * hf, ch * hc
    lane_blocks = lon // TILE_L
    shares = (rf // TILE_R) * lane_blocks
    holders = n_p * rc // TILE_R
    piece = rc // holders
    total = offs.shape[1]
    group = (me // shares) * shares
    rank = me - group

    def holder(c):
        return c * (shares // holders) + (c % 2) * (shares // holders // 2)

    def tile(ref, share):
        row = pl.multiple_of((share // lane_blocks) * TILE_R, TILE_R)
        lane = pl.multiple_of((share % lane_blocks) * TILE_L, TILE_L)
        return ref.at[:, pl.ds(row, TILE_R), pl.ds(lane, TILE_L)]

    def copy_to(src, dst, send, recv, device):
        return pltpu.make_async_remote_copy(
            src_ref=src, dst_ref=dst, send_sem=send, recv_sem=recv,
            device_id=device, device_id_type=pl.DeviceIdType.MESH,
        )

    sources = (fine_h, noise_h, coarse_h, kf_h, kc_h, obs_f_h, obs_c_h, prec_f_h, prec_c_h, offs_h, dest_h)
    places = (fine, noise, coarse, kf, kc, obs_f, obs_c, prec_f, prec_c, offs, dest)
    loads = [pltpu.make_async_copy(a, b, in_sem.at[i]) for i, (a, b) in enumerate(zip(sources, places))]
    for load in loads:
        load.start()

    barrier = pltpu.get_barrier_semaphore()
    for k in range(1, members):
        pl.semaphore_signal(barrier, inc=1, device_id={"ens": lax.rem(me + k, members)},
                            device_id_type=pl.DeviceIdType.MESH)
    for k in range(1, bands):
        pl.semaphore_signal(barrier, inc=1, device_id={"band": lax.rem(band + k, bands)},
                            device_id_type=pl.DeviceIdType.MESH)

    def edge_rows(n_side, rows):
        q = iota((2 * n_side, ch * rows), 0)
        lower = q >= n_side
        t = jnp.where(lower, q - n_side, q)
        depth = jnp.where(t >= ch, 1, 0)
        row = jnp.where(lower, rows - 1 - depth, depth)
        return onehot(iota((2 * n_side, ch * rows), 1) == (t & (ch - 1)) * rows + row)

    sel_state, sel_noise, sel_coarse = edge_rows(2 * ch, hf), edge_rows(ch, hf), edge_rows(2 * ch, hc)
    n_base = n_p * 2 * ch
    c_base = n_base + n_p * ch
    picked_noise = []
    for load in loads[:3]:
        load.wait()
    for p in range(n_p):
        rows = mm(sel_state, fine[p]).astype(BF16)
        halo_tx[0, pl.ds(p * 2 * ch, 2 * ch), :] = rows[: 2 * ch]
        halo_tx[1, pl.ds(p * 2 * ch, 2 * ch), :] = rows[2 * ch :]
        picked_noise.append(mm(sel_noise, noise[0, p]))
    for side in range(2):
        halo_tx[side, pl.ds(n_base, n_p * ch), :] = jnp.concatenate(
            [v[side * ch : (side + 1) * ch] for v in picked_noise], axis=0
        ).astype(BF16)
    c0 = jnp.concatenate([coarse[pl.ds(p * rc, rc), :] for p in range(n_p)], axis=1)
    rows = mm(sel_coarse, c0).astype(BF16)
    halo_tx[0, pl.ds(c_base, 2 * ch), :] = rows[: 2 * ch]
    halo_tx[1, pl.ds(c_base, 2 * ch), :] = rows[2 * ch :]

    pl.semaphore_wait(barrier, members + bands - 2)

    up, down = lax.max(band - 1, 0), lax.min(band + 1, bands - 1)
    has_up, has_down = band > 0, band < bands - 1

    def pair(tx, rx, send, recv, side):
        return copy_to(tx.at[side], rx.at[1 - side], send.at[side], recv.at[1 - side],
                       {"band": up if side == 0 else down})

    halo = [pair(halo_tx, halo_rx, h_send, h_recv, side) for side in range(2)]
    edge = [pair(edge_tx, edge_rx, e_send, e_recv, side) for side in range(2)]

    @pl.when(has_up)
    def _():
        halo[0].start()

    @pl.when(has_down)
    def _():
        halo[1].start()

    r4 = hf // hc
    q = iota((rc + 2 * ch, rf), 0)
    cell_c = jnp.where(q < rc, q >> int(math.log2(hc)), (q - rc) & (ch - 1))
    cell_r = jnp.where(q < rc, q & (hc - 1), jnp.where(q < rc + ch, 0, hc - 1))
    src = iota((rc + 2 * ch, rf), 1)
    gather_rows = onehot((src >> int(math.log2(r4))) == cell_c * hc + cell_r)
    l4 = lon // lonc
    fold = onehot((iota((lon, lonc), 0) >> int(math.log2(l4))) == iota((lon, lonc), 1))
    sums = jnp.concatenate(
        [mm(gather_rows, noise[s, p]) for s in range(2) for p in range(n_p)], axis=0
    )
    hi = sums.astype(BF16)
    rest = sums - hi.astype(F32)
    mid = rest.astype(BF16)
    low = (rest - mid.astype(F32)).astype(BF16)
    scale_r = 4.0 / (r4 * l4)
    folded = (mm(hi, fold) + (mm(mid, fold) + mm(low, fold))) * scale_r
    block = rc + 2 * ch

    def forcing_rows(step, lo, n):
        return jnp.concatenate(
            [folded[(step * n_p + p) * block + lo : (step * n_p + p) * block + lo + n] for p in range(n_p)],
            axis=1,
        )

    edge_tx[0] = forcing_rows(0, rc, ch)
    edge_tx[1] = forcing_rows(0, rc + ch, ch)

    @pl.when(has_up)
    def _():
        edge[0].start()

    @pl.when(has_down)
    def _():
        edge[1].start()

    for load in loads[3:]:
        load.wait()
    lane_w = par_v.shape[1]
    lanes = iota((total, total), 1)
    subs = iota((total, total), 0)
    ends = jnp.sum(jnp.where(lanes <= subs, offs[...], 0), axis=1, keepdims=True)
    parent = jnp.sum(jnp.where(ends <= lanes, 1, 0), axis=0, keepdims=True)
    slot_col = jnp.sum(jnp.where(dest[...] == subs, parent, 0), axis=1, keepdims=True)
    par_v[...] = jnp.sum(
        jnp.where(iota((total, lane_w), 0) == iota((total, lane_w), 1), jnp.minimum(slot_col, total - 1), 0),
        axis=0, keepdims=True,
    )
    to_smem = pltpu.make_async_copy(par_v, par_s, loc.at[0])
    to_smem.start()

    w1 = conv_matrix(kf[...], ch, hf, 1, 2)
    w2 = conv_matrix(kf[...], ch, hf, 0, 1)
    w1c = conv_matrix(kc[...], ch, hc, 1, 2)
    w2c = conv_matrix(kc[...], ch, hc, 0, 1)
    pf = jnp.sum(jnp.where(iota((rf, hf), 1) == (iota((rf, hf), 0) & (hf - 1)), prec_f[...], 0.0), axis=1, keepdims=True)
    pc = jnp.sum(jnp.where(iota((rc, hc), 1) == (iota((rc, hc), 0) & (hc - 1)), prec_c[...], 0.0), axis=1, keepdims=True)
    to_smem.wait()

    @pl.when(jnp.logical_not(has_up))
    def _():
        halo_rx[0] = jnp.zeros(halo_rx.shape[1:], BF16)
        edge_rx[0] = jnp.zeros(edge_rx.shape[1:], F32)

    @pl.when(jnp.logical_not(has_down))
    def _():
        halo_rx[1] = jnp.zeros(halo_rx.shape[1:], BF16)
        edge_rx[1] = jnp.zeros(edge_rx.shape[1:], F32)

    def pair_wait(pairs, which):
        for side in range(2):
            @pl.when((has_up, has_down)[side])
            def _():
                if which == "recv":
                    pairs[1 - side].wait_recv()
                else:
                    pairs[side].wait_send()

    pair_wait(halo, "recv")

    q = iota((ch * (hf + 2), 1), 0)
    keep_f = jnp.logical_and(
        jnp.logical_or(has_up, jnp.logical_or(q < rf, q >= rf + ch)), jnp.logical_or(has_down, q < rf + ch)
    )
    q = iota((ch * (hc + 2), 1), 0)
    keep_c = jnp.logical_and(
        jnp.logical_or(has_up, jnp.logical_or(q < rc, q >= rc + ch)), jnp.logical_or(has_down, q < rc + ch)
    )

    def two_steps(own, above, below, force0, force1, wa, wb, keep, width):
        x = jnp.concatenate([own, above, below], axis=0)
        mixed = mm(wa, shifted(x, width))
        base = jnp.concatenate([own, above[:ch], below[:ch]], axis=0)
        y = (base + 0.5 * jnp.tanh(mixed + force0)).astype(BF16).astype(F32)
        y = jnp.where(keep, y, 0.0)
        mixed = mm(wb, shifted(y, width))
        return (y[: own.shape[0]] + 0.5 * jnp.tanh(mixed + force1)).astype(BF16)

    lane = iota((1, TILE_L), 1)
    like = jnp.zeros((1, TILE_L), F32)
    scale_f = -0.5 / math.sqrt(ch * hf * bands * lon)
    scale_c = -0.5 / math.sqrt(ch * hc * bands * lonc)

    send1, own1 = [], []
    batch = 1
    part1 = lambda ref, first, b: ref.at[pl.ds(first * n_p + b * batch, batch)]

    def share1(share, b):
        row = pl.multiple_of((share // lane_blocks) * TILE_R, TILE_R)
        at = pl.multiple_of((share % lane_blocks) * TILE_L, TILE_L)
        return fin.at[pl.ds(b * batch, batch), pl.ds(row, TILE_R), pl.ds(at, TILE_L)]

    for p in range(n_p):
        hs = [halo_rx[side, pl.ds(p * 2 * ch, 2 * ch), :].astype(F32) for side in range(2)]
        ns = [halo_rx[side, pl.ds(n_base + (p // 2) * 2 * ch, 2 * ch), :].astype(F32)[(p % 2) * ch : (p % 2 + 1) * ch]
              for side in range(2)]
        force0 = jnp.concatenate([noise[0, p].astype(F32), ns[0], ns[1]], axis=0)
        new = two_steps(fine[p].astype(F32), hs[0], hs[1], force0, noise[1, p].astype(F32), w1, w2, keep_f, lon)
        fin[p] = new
        diff = new.astype(F32) - obs_f[...].astype(F32)
        rows = jnp.sum(diff * diff, axis=1, keepdims=True)
        like = like + jnp.where(lane == p, scale_f * jnp.sum(rows * pf, axis=0, keepdims=True), 0.0)

        if (p + 1) % batch == 0:
            b = p // batch
            for k in far_first(members):
                peer = lax.rem(me + k, members)
                send1.append(copy_to(share1(lax.rem(peer, shares), b), part1(recv1, me, b),
                                     s1.at[b * members + k], r1.at[b * members + k], {"ens": peer}))
                send1[-1].start()
            own1.append(pltpu.make_async_copy(share1(rank, b), part1(recv1, me, b), loc.at[2 + b]))
            own1[-1].start()

    pair_wait(edge, "recv")
    hs = [halo_rx[side, pl.ds(c_base, 2 * ch), :].astype(F32) for side in range(2)]
    force0 = jnp.concatenate([forcing_rows(0, 0, rc), edge_rx[0], edge_rx[1]], axis=0)
    new = two_steps(c0.astype(F32), hs[0], hs[1], force0, forcing_rows(1, 0, rc), w1c, w2c, keep_c, lonc)
    parts = []
    for p in range(n_p):
        mine = new[:, p * lonc : (p + 1) * lonc]
        parts.append(mine)
        diff = mine.astype(F32) - obs_c[...].astype(F32)
        rows = jnp.sum(diff * diff, axis=1, keepdims=True)
        like = like + jnp.where(lane == n_p + p, scale_c * jnp.sum(rows * pc, axis=0, keepdims=True), 0.0)
    likeb[band] = jnp.broadcast_to(like, likeb.shape[1:])
    send_b = []
    for k in range(1, bands):
        peer = lax.rem(band + k, bands)
        send_b.append(copy_to(likeb.at[band], likeb.at[band], bs.at[k], br.at[k], {"band": peer}))
        send_b[-1].start()

    n = n_p * rc
    lp = int(math.log2(piece))
    q = iota((n, n), 0)
    src = ((q >> lp) & (n_p - 1)) * rc + (q >> int(math.log2(n_p * piece))) * piece + (q & (piece - 1))
    cstage[...] = mm(onehot(iota((n, n), 1) == src), jnp.concatenate(parts, axis=0)).astype(BF16).reshape(cstage.shape)
    send_c = []
    for g in range(members // shares):
        for c in range(holders):
            peer = g * shares + holder(c)
            send_c.append((peer, copy_to(cstage.at[c], recvc.at[pl.ds(me * TILE_R, TILE_R)],
                                         cs1.at[g * holders + c], cr1.at[lax.rem(peer - me + members, members)],
                                         {"ens": peer})))
    for peer, desc in send_c:
        @pl.when(me != peer)
        def _():
            desc.start()

    for c in range(holders):
        @pl.when(rank == holder(c))
        def _():
            own = pltpu.make_async_copy(cstage.at[c], recvc.at[pl.ds(me * TILE_R, TILE_R)], loc.at[1])
            own.start()
            own.wait()

    for k in range(1, bands):
        src_band = lax.rem(band - k + bands, bands)
        copy_to(likeb.at[src_band], likeb.at[src_band], bs.at[k], br.at[k],
                {"band": lax.rem(band + k, bands)}).wait_recv()
    whole = likeb[0]
    for b in range(1, bands):
        whole = whole + likeb[b]
    whole = whole[:1]
    likee[me] = whole
    send_l = []
    for k in range(1, members):
        send_l.append(copy_to(likee.at[me], likee.at[me], ls.at[k], lr.at[k], {"ens": lax.rem(me + k, members)}))
        send_l[-1].start()

    for b in range(n_p // batch):
        own1[b].wait()
        for k in range(1, members):
            copy_to(share1(rank, b), part1(recv1, lax.rem(me - k + members, members), b),
                    s1.at[b * members + k], r1.at[b * members + k],
                    {"ens": lax.rem(me + k, members)}).wait_recv()
    send2 = []
    for k in far_first(shares) + [0]:
        target = lax.rem(rank + k, shares)
        for s in range(n_p):
            slot = target * n_p + s
            chosen[slot] = recv1[par_s[0, group * n_p + slot]]
        from_ref = chosen.at[pl.ds(target * n_p, n_p)]
        if k:
            send2.append(copy_to(from_ref, tile(out_f, rank), s2.at[k], r2.at[k], {"ens": group + target}))
            send2[-1].start()
        else:
            own2 = pltpu.make_async_copy(from_ref, tile(out_f, rank), loc.at[0])
            own2.start()

    is_holder = functools.reduce(jnp.logical_or, [rank == holder(c) for c in range(holders)])
    n_slots = shares * n_p

    @pl.when(is_holder)
    def _():
        want = group * n_p + (iota((n_slots * piece, total), 0) >> lp)
        who = jnp.sum(jnp.where(dest[...] == want, parent, 0), axis=1, keepdims=True)
        inner = iota((n_slots * piece, 1), 0) & (piece - 1)
        pick = onehot(iota((n_slots * piece, total * piece), 1) == who * piece + inner)
        for k in range(1, members):
            copy_to(cstage.at[0], recvc.at[pl.ds(lax.rem(me - k + members, members) * TILE_R, TILE_R)],
                    cs1.at[0], cr1.at[k], {"ens": lax.rem(me + k, members)}).wait_recv()
        cchosen[...] = mm(pick, recvc[...]).astype(BF16).reshape(cchosen.shape)

    for c in range(holders):
        @pl.when(rank == holder(c))
        def _():
            for k in range(1, shares):
                target = lax.rem(rank + k, shares)
                copy_to(cchosen.at[target], recvc2.at[pl.ds(c * TILE_R, TILE_R)], cs2.at[k], cr2.at[c],
                        {"ens": group + target}).start()
            own = pltpu.make_async_copy(cchosen.at[rank], recvc2.at[pl.ds(c * TILE_R, TILE_R)], loc.at[1])
            own.start()
            own.wait()

    for k in range(1, members):
        src_m = lax.rem(me - k + members, members)
        copy_to(likee.at[src_m], likee.at[src_m], ls.at[k], lr.at[k], {"ens": lax.rem(me + k, members)}).wait_recv()
    everyone = likee[...].reshape(members, TILE_L)
    lane_all = iota((members, TILE_L), 1)
    for first, out in ((0, out_lf), (n_p, out_lc)):
        here = jnp.logical_and(lane_all >= first, lane_all < first + n_p)
        vals = jnp.where(here, everyone, -jnp.inf)
        peak = jnp.max(jnp.max(vals, axis=1, keepdims=True), axis=0, keepdims=True)
        part = jnp.where(here, jnp.exp(vals - peak), 0.0)
        norm = jnp.sum(jnp.sum(part, axis=1, keepdims=True), axis=0, keepdims=True)
        out[...] = (whole - (peak + jnp.log(norm)))[:, first : first + n_p]

    for c in range(holders):
        @pl.when(rank != holder(c))
        def _():
            copy_to(cchosen.at[0], recvc2.at[pl.ds(c * TILE_R, TILE_R)], cs2.at[0], cr2.at[c],
                    {"ens": group + holder(c)}).wait_recv()
    q = iota((n, n), 0)
    row = q & (rc - 1)
    src = (row >> lp) * (n_p * piece) + (q >> int(math.log2(rc))) * piece + (row & (piece - 1))
    out_c[...] = mm(onehot(iota((n, n), 1) == src), recvc2[...]).astype(BF16)

    own2.wait()
    for k in range(1, shares):
        source = lax.rem(rank - k + shares, shares)
        copy_to(chosen.at[pl.ds(0, n_p)], tile(out_f, source), s2.at[k], r2.at[k],
                {"ens": group + lax.rem(rank + k, shares)}).wait_recv()

    pair_wait(halo, "send")
    pair_wait(edge, "send")
    for desc in send1 + send2 + send_b + send_l:
        desc.wait_send()
    for peer, desc in send_c:
        @pl.when(me != peer)
        def _():
            desc.wait_send()

    @pl.when(is_holder)
    def _():
        for k in range(1, shares):
            copy_to(cchosen.at[0], recvc2.at[pl.ds(0, TILE_R)], cs2.at[k], cr2.at[0],
                    {"ens": group + lax.rem(rank + k, shares)}).wait_send()


def write_out(*refs):
    count = (len(refs) - 1) // 2
    copies = [pltpu.make_async_copy(refs[i], refs[count + i], refs[-1].at[i]) for i in range(count)]
    for copy in copies:
        copy.start()
    for copy in copies:
        copy.wait()


def shards(fine, coarse, noise, kf, kc, obs_f, obs_c, prec_f, prec_c, offspring, dest_slot):
    bands, members = lax.axis_size("band"), lax.axis_size("ens")
    n_p, ch, hf, lon = fine.shape
    hc, lonc = coarse.shape[2:]
    rf, rc = ch * hf, ch * hc
    total = offspring.shape[0]
    shares = (rf // TILE_R) * (lon // TILE_L)
    holders = n_p * rc // TILE_R
    groups = members // shares
    lane_w = -(-total // TILE_L) * TILE_L
    halo_rows = n_p * 3 * ch + 2 * ch
    dma = pltpu.SemaphoreType.DMA
    vmem = pl.BlockSpec(memory_space=pltpu.VMEM)
    hbm = pl.BlockSpec(memory_space=pl.ANY)
    args = (
        fine.reshape(n_p, rf, lon),
        coarse.reshape(n_p * rc, lonc),
        noise.reshape(2, n_p, rf, lon),
        kf, kc,
        obs_f.reshape(rf, lon),
        obs_c.reshape(rc, lonc),
        prec_f.reshape(1, hf),
        prec_c.reshape(1, hc),
        offspring.reshape(1, total),
        dest_slot.reshape(1, total),
    )
    results = (
        jax.ShapeDtypeStruct((n_p, rf, lon), BF16),
        jax.ShapeDtypeStruct((n_p * rc, lonc), BF16),
        jax.ShapeDtypeStruct((1, n_p), F32),
        jax.ShapeDtypeStruct((1, n_p), F32),
    )
    done = pl.pallas_call(
        functools.partial(kernel, bands, members),
        out_shape=tuple(pltpu.VMEM(r.shape, r.dtype) for r in results),
        in_specs=[hbm] * 11,
        out_specs=(vmem,) * 4,
        scratch_shapes=[pltpu.VMEM(a.shape, a.dtype) for a in args] + [
            dma((11,)),
            pltpu.VMEM((2, halo_rows, lon), BF16),
            pltpu.VMEM((2, halo_rows, lon), BF16),
            pltpu.VMEM((2, ch, n_p * lonc), F32),
            pltpu.VMEM((2, ch, n_p * lonc), F32),
            pltpu.VMEM((n_p, rf, lon), BF16),
            pltpu.VMEM((total, TILE_R, TILE_L), BF16),
            pltpu.VMEM((shares * n_p, TILE_R, TILE_L), BF16),
            pltpu.VMEM((holders, TILE_R, TILE_L), BF16),
            pltpu.VMEM((members * TILE_R, TILE_L), BF16),
            pltpu.VMEM((shares, TILE_R, TILE_L), BF16),
            pltpu.VMEM((holders * TILE_R, TILE_L), BF16),
            pltpu.VMEM((bands, 8, TILE_L), F32),
            pltpu.VMEM((members, 1, TILE_L), F32),
            pltpu.VMEM((1, lane_w), I32),
            pltpu.SMEM((1, lane_w), I32),
            dma((2,)), dma((2,)), dma((2,)), dma((2,)),
            dma((n_p * members,)), dma((n_p * members,)), dma((shares,)), dma((shares,)),
            dma((groups * holders,)), dma((members,)), dma((shares,)), dma((holders,)),
            dma((bands,)), dma((bands,)), dma((members,)), dma((members,)), dma((2 + n_p,)),
        ],
        compiler_params=pltpu.CompilerParams(
            collective_id=0, has_side_effects=True, vmem_limit_bytes=VMEM_LIMIT
        ),
    )(*args)
    of, oc, lf, lc = pl.pallas_call(
        write_out,
        out_shape=results,
        in_specs=[vmem] * 4,
        out_specs=(hbm,) * 4,
        scratch_shapes=[dma((4,))],
        compiler_params=pltpu.CompilerParams(vmem_limit_bytes=4 * 1024 * 1024),
    )(*[pltpu.with_memory_space_constraint(d, pltpu.VMEM) for d in done])
    return (
        of.reshape(n_p, ch, hf, lon),
        oc.reshape(n_p, ch, hc, lonc),
        lf.reshape(n_p),
        lc.reshape(n_p),
    )


def solution(mesh):
    return jax.shard_map(
        shards,
        mesh=mesh,
        in_specs=(
            P("ens", None, "band", None),
            P("ens", None, "band", None),
            P(None, "ens", None, "band", None),
            P(),
            P(),
            P(None, "band", None),
            P(None, "band", None),
            P("band"),
            P("band"),
            P(),
            P(),
        ),
        out_specs=(P("ens", None, "band", None), P("ens", None, "band", None), P("ens"), P("ens")),
        check_vma=False,
    )
```
